128 devices in a mesh: dp: 4 (over y_hi, core), seq: 32 (over x, y_lo, z).
Axes of the slice: x: 4, y: 4 (y_hi: 2, y_lo: 2; y = y_hi * 2 + y_lo), z: 4, core: 2. Of those that a mesh axis runs over, the one named last changes fastest.
Arguments:
- query_in: bfloat16 [4, 4096, 2048], P('dp', 'seq'), may hold values from -6 to 6
- key_in: bfloat16 [4, 4096, 2048], P('dp', 'seq'), may hold values from -6 to 6
- value_in: bfloat16 [4, 4096, 2048], P('dp', 'seq'), may hold values from -6 to 6
- grad_out: bfloat16 [4, 4096, 2048], P('dp', 'seq'), may hold values from -6 to 6
- filter_taps: float32 [2048, 4096], P('seq'), may hold values from -2 to 2
Outputs:
- grad_query: bfloat16 [4, 4096, 2048], P('dp', 'seq')
- grad_key: bfloat16 [4, 4096, 2048], P('dp', 'seq')
- grad_value: bfloat16 [4, 4096, 2048], P('dp', 'seq')
- grad_filter: float32 [2048, 4096], P('seq', 'dp')
The draws below stay inside these ranges and needn't reach their ends.
All inputs are finite; a program needn't handle non-finite values.
Results may differ from the reference program's by a relative error of at most 0.013.
Values may be sent and summed in bfloat16 or wider, within the bound.
No kernel may reach another device: no remote copies, remote signals or barrier semaphores. Data moves between devices by JAX's collectives and lax.ppermute only.
A program may use at most 64 MiB of HBM per device.

```python
import jax
import jax.numpy as jnp
from jax import lax

C = 2048
L = 4096
SEQS = 4


def draw_filter_taps(key, part):
    key = jax.random.fold_in(key, 7)
    key_pick, key_rate, key_noise = jax.random.split(key, 3)
    length_f = jnp.float32(L)
    pick = jax.random.uniform(key_pick, (C, 1), jnp.float32)
    spot = jax.random.uniform(key_rate, (C, 1), jnp.float32)
    slow_lo = jnp.log(0.25 / length_f)
    slow_hi = jnp.log(2.0 / length_f)
    fast_lo = jnp.log(2.0 / length_f)
    fast_hi = jnp.log(1.0 / 30.0)
    slow_rate = jnp.exp(slow_lo + spot * (slow_hi - slow_lo))
    fast_rate = jnp.exp(fast_lo + spot * (fast_hi - fast_lo))
    rate = jnp.where(pick < 0.5, fast_rate, slow_rate)
    noise = jnp.clip(jax.random.normal(key_noise, (C, L), jnp.float32), -6.0, 6.0)
    taps = jnp.arange(L, dtype=jnp.float32)[None, :]
    scale = jnp.sqrt((1.0 - jnp.exp(-2.0 * rate)) / (1.0 - jnp.exp(-2.0 * rate * length_f)))
    return noise * scale * jnp.exp(-rate * taps)


def level_of(rng, dims, cuts, least, high):
    def one(position, shards_of):
        heights = jax.random.uniform(jax.random.fold_in(jax.random.fold_in(rng, 6), position), (shards_of,), jnp.float32, least / len(cuts), high / len(cuts))
        return jnp.repeat(jnp.exp(heights), dims[position] // shards_of).reshape((-1,) + (1,) * (len(dims) - position - 1))

    loudness = one(*cuts[0])
    for cut in cuts[1:]:
        loudness = loudness * one(*cut)
    return loudness


def bell_draw(key, shape, spread, bound, shards=(), kind=jnp.bfloat16):
    drawn = jax.random.normal(key, shape, jnp.float32) * spread
    if len(shards) > 0:
        drawn = level_of(key, shape, shards, -0.22, 0.18) * drawn
    return jnp.clip(drawn, min=-bound, max=bound).astype(kind)


def setup_inputs(seed: int = 0) -> dict:
    streams_of = jax.random.split(jax.random.key(seed), 6)
    return {
        "query_in": bell_draw(streams_of[0], (SEQS, L, C), 1.0, 6.0, ((0, 4), (1, 32))),
        "key_in": bell_draw(streams_of[1], (SEQS, L, C), 1.0, 6.0, ((0, 4), (1, 32))),
        "value_in": bell_draw(streams_of[2], (SEQS, L, C), 1.0, 6.0, ((0, 4), (1, 32))),
        "grad_out": bell_draw(streams_of[3], (SEQS, L, C), 1.0, 6.0, ((0, 4), (1, 32))),
        "filter_taps": draw_filter_taps(jax.random.fold_in(streams_of[5], 71), 0),
    }


def reference(query_in, key_in, value_in, grad_out, filter_taps):
    length = query_in.shape[1]
    full = 2 * length
    filt_spec = jnp.fft.rfft(filter_taps.T, n=full, axis=0)

    def one_seq(carry, items):
        query, keys, values, cotan = items
        gated = (keys.astype(jnp.float32) * values.astype(jnp.float32)).astype(jnp.bfloat16)
        conv_grad = (query.astype(jnp.float32) * cotan.astype(jnp.float32)).astype(jnp.bfloat16)
        gated_spec = jnp.fft.rfft(gated.astype(jnp.float32), n=full, axis=0)
        grad_spec = jnp.fft.rfft(conv_grad.astype(jnp.float32), n=full, axis=0)
        conv_out = jnp.fft.irfft(filt_spec * gated_spec, n=full, axis=0)[:length].astype(jnp.bfloat16)
        gated_grad = jnp.fft.irfft(jnp.conj(filt_spec) * grad_spec, n=full, axis=0)[:length].astype(jnp.bfloat16)
        filt_term = jnp.fft.irfft(grad_spec * jnp.conj(gated_spec), n=full, axis=0)[:length]
        grad_query = (cotan.astype(jnp.float32) * conv_out.astype(jnp.float32)).astype(jnp.bfloat16)
        grad_key = (gated_grad.astype(jnp.float32) * values.astype(jnp.float32)).astype(jnp.bfloat16)
        grad_value = (gated_grad.astype(jnp.float32) * keys.astype(jnp.float32)).astype(jnp.bfloat16)
        return (carry + filt_term.astype(carry.dtype), (grad_query, grad_key, grad_value))
    start = jnp.zeros((length, filter_taps.shape[0]), jnp.float32)
    total, grads = lax.scan(one_seq, start, (query_in, key_in, value_in, grad_out))
    scale = lax.rsqrt(jnp.float32(query_in.shape[0] * length))
    return (grads[0], grads[1], grads[2], total.T * scale)
```

```python
import functools

import jax
import jax.numpy as jnp
import ml_dtypes
import numpy as np
from jax import lax
from jax.experimental import pallas as pl
from jax.experimental.pallas import tpu as pltpu
from jax.sharding import PartitionSpec as P

TOKENS = 4096
ROWS = 32
COLS = 128
LANES = 128
HALF = 64
SUB = 8
GROUPS = COLS // SUB
F32 = jnp.float32
BF16 = jnp.bfloat16
VMEM_LIMIT = 48 * 1024 * 1024


@functools.cache
def tables():
    index = np.arange(ROWS)
    token = COLS * index[:, None] + np.arange(COLS)[None, :]
    angle = 2.0 * np.pi * (index[:, None, None] + 0.25) * token[None] / TOKENS
    parts = np.stack([np.cos(angle), -np.sin(angle)])
    parts = parts.reshape(2, ROWS, ROWS, GROUPS, SUB)
    eye = np.eye(SUB)
    first = np.einsum("akpgr,rs->gakrps", parts, eye).reshape(GROUPS, 2 * ROWS * SUB, ROWS * SUB)
    last = np.swapaxes(first, 1, 2) / TOKENS
    turn = 2.0 * np.pi * (np.arange(COLS)[:, None] * np.arange(COLS)[None, :] % COLS) / COLS
    cos, sin = np.cos(turn), np.sin(turn)
    ahead = np.block([[cos, sin], [-sin, cos]])
    back = np.block([[cos, -sin], [sin, cos]])
    kind = ml_dtypes.bfloat16
    return tuple(table.astype(kind) for table in (first, last, ahead, back))


def dot(left, right):
    return jnp.dot(left, right, preferred_element_type=F32)


def lane_low(shape):
    return lax.broadcasted_iota(jnp.int32, shape, len(shape) - 1) < HALF


def swap_halves(block):
    return pltpu.roll(block, HALF, block.ndim - 1)


def split_rows(block, count):
    wide = block.astype(F32)
    low = wide[:, :SUB].reshape(count * SUB, LANES).astype(BF16)
    high = wide[:, SUB:].reshape(count * SUB, LANES).astype(BF16)
    return low, high


def join_rows(low, high, count):
    shape = (count, SUB, LANES)
    return jnp.concatenate([low.reshape(shape), high.reshape(shape)], axis=1)


def first_step(source, first_ref, spread_ref):
    @pl.loop(0, GROUPS // 2)
    def _(step):
        rows = pl.ds(pl.multiple_of(step * 2 * SUB, 2 * SUB), 2 * SUB)
        low, high = split_rows(source[:, rows, :], ROWS)
        joined = join_rows(dot(first_ref[2 * step], low), dot(first_ref[2 * step + 1], high), 2 * ROWS)
        spread_ref[:, rows, :] = joined.astype(BF16)


def last_step(spread_ref, last_ref, store):
    @pl.loop(0, GROUPS // 2)
    def _(step):
        rows = pl.ds(pl.multiple_of(step * 2 * SUB, 2 * SUB), 2 * SUB)
        low, high = split_rows(spread_ref[:, rows, :], 2 * ROWS)
        store(rows, join_rows(dot(last_ref[2 * step], low), dot(last_ref[2 * step + 1], high), ROWS))


def pair_of(spread_ref, step):
    sides = []
    for k in (2 * step, 2 * step + 1):
        sides.append(jnp.concatenate([spread_ref[k], spread_ref[ROWS + k]], axis=0))
    return jnp.concatenate(sides, axis=1)


def gate_kernel(query_ref, key_ref, value_ref, cotan_ref, out_ref):
    low = lane_low((COLS, LANES))
    for block in range(out_ref.shape[0] // 2):
        lanes = pl.ds(block * LANES, LANES)
        gated = key_ref[:, lanes].astype(F32) * value_ref[:, lanes].astype(F32)
        grad = query_ref[:, lanes].astype(F32) * cotan_ref[:, lanes].astype(F32)
        out_ref[2 * block] = jnp.where(low, gated, swap_halves(grad)).astype(BF16)
        out_ref[2 * block + 1] = jnp.where(low, swap_halves(gated), grad).astype(BF16)


def filter_kernel(taps_ref, first_ref, ahead_ref, real_ref, imag_ref, rows_ref, spread_ref):
    for p in range(ROWS):
        block = taps_ref[:, p * COLS : (p + 1) * COLS]
        rows_ref[p] = jnp.concatenate([block, block], axis=0).T.astype(BF16)
    first_step(rows_ref, first_ref, spread_ref)
    low = lane_low((COLS, LANES))

    @pl.loop(0, ROWS // 2)
    def _(step):
        spec = dot(ahead_ref[...], pair_of(spread_ref, step))
        for side in range(2):
            part = spec[:, side * LANES : (side + 1) * LANES]
            real_ref[2 * step + side] = part[:COLS]
            imag_ref[2 * step + side] = jnp.where(low, part[COLS:], -part[COLS:])


def conv_kernel(data_ref, filt_re, filt_im, first_ref, last_ref, ahead_ref, back_ref, out_ref, spec_ref, spread_ref):
    first_step(data_ref, first_ref, spread_ref)

    @pl.loop(0, ROWS // 2)
    def _(step):
        spec = dot(ahead_ref[...], pair_of(spread_ref, step))
        sides = []
        for side in range(2):
            k = 2 * step + side
            real = spec[:COLS, side * LANES : (side + 1) * LANES]
            imag = spec[COLS:, side * LANES : (side + 1) * LANES]
            spec_ref[k] = real
            spec_ref[ROWS + k] = imag
            turn_re, turn_im = filt_re[k], filt_im[k]
            prod_re = turn_re * real - turn_im * imag
            prod_im = turn_re * imag + turn_im * real
            sides.append(jnp.concatenate([prod_re, prod_im], axis=0).astype(BF16))
        result = dot(back_ref[...], jnp.concatenate(sides, axis=1)).astype(BF16)
        for side in range(2):
            k = 2 * step + side
            spread_ref[k] = result[:COLS, side * LANES : (side + 1) * LANES]
            spread_ref[ROWS + k] = result[COLS:, side * LANES : (side + 1) * LANES]

    def store(rows, block):
        out_ref[:, rows, :] = block.astype(BF16)

    last_step(spread_ref, last_ref, store)


def taps_kernel(place_ref, spec_ref, last_ref, back_ref, out_ref, spread_ref, lags_ref):
    @pl.loop(0, ROWS // 2)
    def _(step):
        sides = []
        for side in range(2):
            k = 2 * step + side
            real, imag = spec_ref[k], spec_ref[ROWS + k]
            other_re, other_im = swap_halves(real), swap_halves(imag)
            prod_re = other_re * real + other_im * imag
            prod_im = other_im * real - other_re * imag
            sides.append(jnp.concatenate([prod_re, prod_im], axis=0).astype(BF16))
        result = dot(back_ref[...], jnp.concatenate(sides, axis=1)).astype(BF16)
        for side in range(2):
            k = 2 * step + side
            spread_ref[k] = result[:COLS, side * LANES : (side + 1) * LANES]
            spread_ref[ROWS + k] = result[COLS:, side * LANES : (side + 1) * LANES]

    def store(rows, block):
        lags_ref[:, rows, :] = block

    last_step(spread_ref, last_ref, store)
    place = place_ref[0]
    per = ROWS // 4
    for quarter in range(4):
        slot = jnp.bitwise_xor(place, quarter)
        for p in range(per):
            out_ref[slot, :, p * COLS : (p + 1) * COLS] = lags_ref[quarter * per + p].T[:HALF].astype(BF16)


def mix_kernel(data_ref, key_ref, value_ref, cotan_ref, query_out, key_out, value_out):
    low = lane_low((COLS, LANES))
    for block in range(data_ref.shape[0] // 2):
        lanes = pl.ds(block * LANES, LANES)
        even = data_ref[2 * block].astype(F32)
        odd = data_ref[2 * block + 1].astype(F32)
        conv = jnp.where(low, even, swap_halves(odd))
        grad = jnp.where(low, swap_halves(even), odd)
        query_out[:, lanes] = (cotan_ref[:, lanes].astype(F32) * conv).astype(BF16)
        key_out[:, lanes] = (grad * value_ref[:, lanes].astype(F32)).astype(BF16)
        value_out[:, lanes] = (grad * key_ref[:, lanes].astype(F32)).astype(BF16)


def call(kernel, out_shape, scratch=(), flops=0, nbytes=0, smem=0):
    inside = pl.BlockSpec(memory_space=pltpu.VMEM)
    scalar = pl.BlockSpec(memory_space=pltpu.SMEM)

    def run(*args):
        return pl.pallas_call(
            kernel,
            out_shape=out_shape,
            in_specs=[scalar] * smem + [inside] * (len(args) - smem),
            out_specs=jax.tree.map(lambda _: inside, out_shape),
            scratch_shapes=list(scratch),
            compiler_params=pltpu.CompilerParams(vmem_limit_bytes=VMEM_LIMIT),
            cost_estimate=pl.CostEstimate(flops=flops, bytes_accessed=nbytes, transcendentals=0),
        )(*args)

    return run


def on_device(query_in, key_in, value_in, grad_out, filter_taps):
    first, last, ahead, back = (jnp.asarray(table) for table in tables())
    query, keys, values, cotan = query_in[0], key_in[0], value_in[0], grad_out[0]
    shape = jax.ShapeDtypeStruct
    cube = (ROWS, COLS, LANES)
    unit = 2 * 16 * 512 * 256 * 128
    spread = pltpu.VMEM((2 * ROWS, COLS, LANES), BF16)

    sent = call(gate_kernel, shape(cube, BF16), flops=1 << 21, nbytes=3 << 20)(query, keys, values, cotan)
    filt_re, filt_im = call(
        filter_kernel,
        (shape(cube, F32), shape(cube, F32)),
        [pltpu.VMEM(cube, BF16), spread],
        flops=2 * unit,
        nbytes=10 << 20,
    )(filter_taps, first, ahead)
    data = lax.all_to_all(sent, "seq", split_axis=0, concat_axis=0, tiled=True)
    result, spec = call(
        conv_kernel,
        (shape(cube, BF16), shape((2 * ROWS, COLS, LANES), F32)),
        [spread],
        flops=4 * unit,
        nbytes=18 << 20,
    )(data, filt_re, filt_im, first, last, ahead, back)
    returned = lax.all_to_all(result, "seq", split_axis=0, concat_axis=0, tiled=True)
    place = lax.axis_index("dp").astype(jnp.int32).reshape(1)
    terms = call(
        taps_kernel,
        shape((4, HALF, TOKENS // 4), BF16),
        [spread, pltpu.VMEM(cube, F32)],
        flops=2 * unit,
        nbytes=9 << 20,
        smem=1,
    )(place, spec, last, back)
    total = terms[0].astype(F32)
    for shift in range(1, 4):
        pairs = [(d, d ^ shift) for d in range(4)]
        total = total + lax.ppermute(terms[shift], "dp", pairs).astype(F32)
    grad_filter = total * lax.rsqrt(F32(4 * TOKENS))
    wide = shape(query.shape, BF16)
    grad_query, grad_key, grad_value = call(
        mix_kernel, (wide, wide, wide), flops=1 << 21, nbytes=4 << 20
    )(returned, keys, values, cotan)
    return (grad_query[None], grad_key[None], grad_value[None], grad_filter)


def solution(mesh):
    tokens = P("dp", "seq", None)
    return jax.shard_map(
        on_device,
        mesh=mesh,
        in_specs=(tokens, tokens, tokens, tokens, P("seq", None)),
        out_specs=(tokens, tokens, tokens, P("seq", "dp")),
        check_vma=False,
    )
```

```python
import functools
import math

import jax
import jax.numpy as jnp
import ml_dtypes
import numpy as np
from jax import lax
from jax.experimental import pallas as pl
from jax.experimental.pallas import tpu as pltpu
from jax.sharding import PartitionSpec as P

TOKENS = 4096
ROWS = 32
COLS = 128
OWN = 64
SUB = 8
PAIR = 2 * SUB
BLOCK = ROWS * SUB
F32 = jnp.float32
BF16 = jnp.bfloat16
CHUNKS = 4
STEPS = OWN // PAIR
VMEM_LIMIT = 63 * 1024 * 1024


@functools.cache
def tables():
    index = np.arange(ROWS)
    rate = index + 0.25
    angle = 2.0 * np.pi * rate[:, None] * index[None, :] / ROWS
    parts = np.concatenate([np.cos(angle), -np.sin(angle)])
    first = np.kron(parts, np.eye(SUB))
    last = first.T / TOKENS
    twist = 2.0 * np.pi * rate[:, None] * np.arange(COLS)[None, :] / TOKENS
    turn = 2.0 * np.pi * (np.arange(COLS)[:, None] * np.arange(COLS)[None, :] % COLS) / COLS
    cos, sin = np.cos(turn), np.sin(turn)
    ahead = np.block([[cos, -sin], [sin, cos]])
    back = np.block([[cos, sin], [-sin, cos]])
    kind = ml_dtypes.bfloat16
    return (
        np.stack([np.cos(twist), np.sin(twist)]).astype(np.float32),
        first.astype(kind),
        ahead.astype(kind),
        last.astype(kind),
        back.astype(kind),
    )


def dot(left, right):
    return jnp.dot(left, right, preferred_element_type=F32)


def both(left, right):
    return jnp.concatenate([left, right], axis=1)


def split_rows(block):
    wide = block.astype(F32)
    low = wide[:, :SUB].reshape(BLOCK, COLS)
    high = wide[:, SUB:].reshape(BLOCK, COLS)
    return both(low, high).astype(BF16)


def tall(table):
    return jnp.broadcast_to(table[:, None, :], (ROWS, SUB, COLS)).reshape(BLOCK, COLS)


def spectrum(rows, twist_ref, first_ref, ahead_ref):
    cos, sin = tall(twist_ref[0]), tall(twist_ref[1])
    wide = dot(first_ref[...], rows)
    specs = []
    for side in range(2):
        lanes = slice(side * COLS, (side + 1) * COLS)
        real, imag = wide[:BLOCK, lanes], wide[BLOCK:, lanes]
        turned = both(real * cos + imag * sin, imag * cos - real * sin)
        specs.append(dot(turned.astype(BF16), ahead_ref[...]))
    return specs


def inverse(specs, twist_ref, last_ref, back_ref):
    cos, sin = tall(twist_ref[0]), tall(twist_ref[1])
    sides = []
    for spec in specs:
        wide = dot(spec.astype(BF16), back_ref[...])
        real, imag = wide[:, :COLS], wide[:, COLS:]
        sides.append(jnp.concatenate([real * cos - imag * sin, imag * cos + real * sin], axis=0))
    wide = dot(last_ref[...], both(*sides).astype(BF16))
    shape = (ROWS, SUB, COLS)
    return jnp.concatenate([wide[:, :COLS].reshape(shape), wide[:, COLS:].reshape(shape)], axis=1)


def product(left, right, conj):
    left_re, left_im = left[:, :COLS].astype(F32), left[:, COLS:].astype(F32)
    right_re, right_im = right[:, :COLS].astype(F32), right[:, COLS:].astype(F32)
    if conj:
        return both(left_re * right_re + left_im * right_im, left_re * right_im - left_im * right_re)
    return both(left_re * right_re - left_im * right_im, left_re * right_im + left_im * right_re)


def copies_of(pairs, sems):
    copies = []
    for place, (source, target) in enumerate(pairs):
        copies.append(pltpu.make_async_copy(source, target, sems.at[place]))
    for copy in copies:
        copy.start()
    return copies


def wait_all(copies):
    for copy in copies:
        copy.wait()


def gate_kernel(query_hbm, key_hbm, value_hbm, cotan_hbm, out_hbm, held, sent, in_sems, out_sems):
    sources = (key_hbm, value_hbm, query_hbm, cotan_hbm)
    span = held.shape[2] // CHUNKS
    pairs = []
    for chunk in range(CHUNKS):
        lanes = pl.ds(chunk * span, span)
        pairs += [(source.at[:, lanes], held.at[place, :, lanes]) for place, source in enumerate(sources)]
    arriving = copies_of(pairs, in_sems)
    leaving = []
    for chunk in range(CHUNKS):
        wait_all(arriving[4 * chunk : 4 * chunk + 4])
        first_block, last_block = chunk * span // COLS, (chunk + 1) * span // COLS
        for block in range(first_block, last_block):
            lanes = pl.ds(block * COLS, COLS)
            for part in range(2):
                left, right = held[2 * part, :, lanes].astype(F32), held[2 * part + 1, :, lanes].astype(F32)
                turned = (left * right).T.astype(BF16)
                rows = slice(part * OWN, (part + 1) * OWN)
                sent[2 * block, rows] = turned[:OWN]
                sent[2 * block + 1, rows] = turned[OWN:]
        dests = pl.ds(2 * first_block, 2 * (last_block - first_block))
        copy = pltpu.make_async_copy(sent.at[dests], out_hbm.at[dests], out_sems.at[chunk])
        copy.start()
        leaving.append(copy)
    wait_all(leaving)


def filter_kernel(
    taps_hbm, twist_hbm, first_hbm, ahead_hbm, out_hbm, taps, twist, first, ahead, filt, sems, out_sems
):
    pairs = [(first_hbm, first), (twist_hbm, twist), (ahead_hbm, ahead)]
    for step in range(STEPS):
        rows = pl.ds(step * PAIR, PAIR)
        pairs.append((taps_hbm.at[rows], taps.at[rows]))
    arriving = copies_of(pairs, sems)
    wait_all(arriving[:3])
    leaving = []
    for step in range(STEPS):
        arriving[3 + step].wait()
        sides = []
        for side in range(2):
            low = (2 * step + side) * SUB
            sides.append(
                jnp.concatenate([taps[low : low + SUB, p * COLS : (p + 1) * COLS] for p in range(ROWS)], axis=0)
            )
        specs = spectrum(both(*sides).astype(BF16), twist, first, ahead)
        for side in range(2):
            filt[2 * step + side] = specs[side].astype(BF16)
        groups = pl.ds(2 * step, 2)
        copy = pltpu.make_async_copy(filt.at[groups], out_hbm.at[groups], out_sems.at[step])
        copy.start()
        leaving.append(copy)
    wait_all(leaving)


def conv_kernel(
    data_hbm,
    filt_hbm,
    twist_hbm,
    first_hbm,
    ahead_hbm,
    last_hbm,
    back_hbm,
    out_hbm,
    cross_hbm,
    data,
    filt,
    twist,
    first,
    ahead,
    last,
    back,
    out,
    cross,
    sems,
    out_sems,
):
    pairs = [(first_hbm, first), (data_hbm, data), (twist_hbm, twist), (ahead_hbm, ahead)]
    pairs += [(filt_hbm, filt), (back_hbm, back), (last_hbm, last)]
    arriving = copies_of(pairs, sems)
    wait_all(arriving)
    leaving = []
    for step in range(STEPS):
        specs = []
        for part in range(2):
            rows = slice(part * OWN + step * PAIR, part * OWN + (step + 1) * PAIR)
            specs.append(spectrum(split_rows(data[:, rows, :]), twist, first, ahead))
        for part in range(2):
            rows = slice(part * OWN + step * PAIR, part * OWN + (step + 1) * PAIR)
            prods = [product(filt[2 * step + side], specs[part][side], part == 1) for side in range(2)]
            out[:, rows, :] = inverse(prods, twist, last, back).astype(BF16)
            leaving += copies_of([(out.at[:, rows, :], out_hbm.at[:, rows, :])], out_sems.at[step, part:])
        for side in range(2):
            cross[2 * step + side] = product(specs[0][side], specs[1][side], True).astype(BF16)
        groups = pl.ds(2 * step, 2)
        leaving += copies_of([(cross.at[groups], cross_hbm.at[groups])], out_sems.at[step, 2:])
    wait_all(leaving)


def taps_kernel(
    place_ref, cross_hbm, twist_hbm, last_hbm, back_hbm, own_hbm, near_hbm, cross, twist, last, back, lags_ref, sems, out_sems
):
    pairs = [(back_hbm, back), (cross_hbm, cross), (twist_hbm, twist), (last_hbm, last)]
    wait_all(copies_of(pairs, sems))
    per = ROWS // 4
    for step in range(STEPS):
        lags = inverse([cross[2 * step + side] for side in range(2)], twist, last, back).astype(BF16)
        rows = slice(step * PAIR, (step + 1) * PAIR)
        for p in range(ROWS):
            lags_ref[p // per, rows, (p % per) * COLS : (p % per + 1) * COLS] = lags[p]
    place = place_ref[0]
    pairs = []
    for shift in range(4):
        target = (own_hbm, near_hbm)[shift % 2]
        pairs.append((lags_ref.at[jnp.bitwise_xor(place, shift)], target.at[shift // 2]))
    wait_all(copies_of(pairs, out_sems))


def mix_kernel(
    data_hbm,
    key_hbm,
    value_hbm,
    cotan_hbm,
    own_hbm,
    near_hbm,
    far_hbm,
    query_out,
    key_out,
    value_out,
    filter_out,
    data,
    held,
    terms,
    grads,
    total,
    sems,
    out_sems,
):
    span = held.shape[2] // CHUNKS
    sources = (cotan_hbm, value_hbm, key_hbm)
    outs = (query_out, key_out, value_out)
    pairs = []
    for chunk in range(CHUNKS):
        dests = pl.ds(2 * chunk * span // COLS, 2 * span // COLS)
        lanes = pl.ds(chunk * span, span)
        pairs.append((data_hbm.at[dests], data.at[dests]))
        pairs += [(source.at[:, lanes], held.at[place, :, lanes]) for place, source in enumerate(sources)]
    pairs += [(source, terms.at[place]) for place, source in enumerate((own_hbm.at[0], near_hbm.at[0], far_hbm))]
    arriving = copies_of(pairs, sems)
    leaving = []
    for chunk in range(CHUNKS):
        wait_all(arriving[4 * chunk : 4 * chunk + 4])
        for block in range(chunk * span // COLS, (chunk + 1) * span // COLS):
            lanes = pl.ds(block * COLS, COLS)
            turned = []
            for part in range(2):
                rows = slice(part * OWN, (part + 1) * OWN)
                tall = jnp.concatenate([data[2 * block, rows], data[2 * block + 1, rows]], axis=0)
                turned.append(tall.astype(F32).T)
            conv, grad = turned
            for place, factor in enumerate((conv, grad, grad)):
                grads[place, :, lanes] = (factor * held[place, :, lanes].astype(F32)).astype(BF16)
        lanes = pl.ds(chunk * span, span)
        pairs = [(grads.at[place, :, lanes], outs[place].at[:, lanes]) for place in range(3)]
        leaving += copies_of(pairs, out_sems.at[chunk])
    wait_all(arriving[4 * CHUNKS :])
    whole = terms[0].astype(F32) + terms[1].astype(F32) + terms[2].astype(F32)
    total[...] = whole * (1.0 / math.sqrt(4 * TOKENS))
    leaving += copies_of([(total, filter_out)], out_sems.at[CHUNKS])
    wait_all(leaving)


def call(kernel, out_shape, scratch=(), flops=0, nbytes=0, smem=0):
    far = pl.BlockSpec(memory_space=pl.ANY)
    scalar = pl.BlockSpec(memory_space=pltpu.SMEM)

    def run(*args):
        return pl.pallas_call(
            kernel,
            out_shape=out_shape,
            in_specs=[scalar] * smem + [far] * (len(args) - smem),
            out_specs=jax.tree.map(lambda _: far, out_shape),
            scratch_shapes=list(scratch),
            compiler_params=pltpu.CompilerParams(vmem_limit_bytes=VMEM_LIMIT),
            cost_estimate=pl.CostEstimate(flops=flops, bytes_accessed=nbytes, transcendentals=0),
        )(*args)

    return run


def swap(array):
    return lax.all_to_all(array, "seq", split_axis=0, concat_axis=0, tiled=True)


def on_device(query_in, key_in, value_in, grad_out, filter_taps):
    twist, first, ahead, last, back = (jnp.asarray(table) for table in tables())
    query, keys, values, cotan = query_in[0], key_in[0], value_in[0], grad_out[0]
    shape = jax.ShapeDtypeStruct
    sems = pltpu.SemaphoreType.DMA
    cube = shape((ROWS, 2 * OWN, COLS), BF16)
    filt_spec = shape((OWN // SUB, BLOCK, 2 * COLS), BF16)
    wide = shape(query.shape, BF16)
    quarter = shape((OWN, TOKENS // 4), BF16)
    unit = 1 << 30

    def room(*arrays):
        return [pltpu.VMEM(array.shape, array.dtype) for array in arrays]

    sent = call(
        gate_kernel,
        cube,
        [pltpu.VMEM((4, *query.shape), BF16), *room(cube), sems((4 * CHUNKS,)), sems((CHUNKS,))],
        flops=1 << 20,
        nbytes=3 << 20,
    )(query, keys, values, cotan)
    filt = call(
        filter_kernel,
        filt_spec,
        [*room(filter_taps, twist, first, ahead, filt_spec), sems((3 + STEPS,)), sems((STEPS,))],
        flops=unit // 2,
        nbytes=3 << 20,
    )(filter_taps, twist, first, ahead)
    data = swap(sent)
    result, cross = call(
        conv_kernel,
        (cube, filt_spec),
        [
            *room(cube, filt_spec, twist, first, ahead, last, back, cube, filt_spec),
            sems((7,)),
            sems((STEPS, 3)),
        ],
        flops=2 * unit,
        nbytes=5 << 20,
    )(data, filt, twist, first, ahead, last, back)
    returned = swap(result)
    place = lax.axis_index("dp").astype(jnp.int32).reshape(1)
    half = shape((2, *quarter.shape), BF16)
    own, sent_near = call(
        taps_kernel,
        (half, half),
        [
            *room(filt_spec, twist, last, back),
            pltpu.VMEM((4, *quarter.shape), BF16),
            sems((4,)),
            sems((4,)),
        ],
        flops=unit // 2,
        nbytes=2 << 20,
        smem=1,
    )(place, cross, twist, last, back)
    near = lax.ppermute(sent_near, "dp", [(d, d ^ 1) for d in range(4)])
    partial = (own[1].astype(F32) + near[1].astype(F32)).astype(BF16)
    far = lax.ppermute(partial, "dp", [(d, d ^ 2) for d in range(4)])
    grad_query, grad_key, grad_value, grad_filter = call(
        mix_kernel,
        (wide, wide, wide, shape(quarter.shape, F32)),
        [
            *room(cube),
            pltpu.VMEM((3, *wide.shape), BF16),
            pltpu.VMEM((3, *quarter.shape), BF16),
            pltpu.VMEM((3, *wide.shape), BF16),
            pltpu.VMEM(quarter.shape, F32),
            sems((4 * CHUNKS + 3,)),
            sems((CHUNKS + 1, 3)),
        ],
        flops=1 << 20,
        nbytes=4 << 20,
    )(returned, keys, values, cotan, own, near, far)
    return (grad_query[None], grad_key[None], grad_value[None], grad_filter)


def solution(mesh):
    tokens = P("dp", "seq", None)
    return jax.shard_map(
        on_device,
        mesh=mesh,
        in_specs=(tokens, tokens, tokens, tokens, P("seq", None)),
        out_specs=(tokens, tokens, tokens, P("seq", "dp")),
        check_vma=False,
    )
```

```python
import functools
import math

import jax
import jax.numpy as jnp
import ml_dtypes
import numpy as np
from jax import lax
from jax.experimental import pallas as pl
from jax.experimental.pallas import tpu as pltpu
from jax.sharding import PartitionSpec as P

TOKENS = 4096
ROWS = 32
COLS = 128
OWN = 64
SUB = 8
PAIR = 2 * SUB
BLOCK = ROWS * SUB
F32 = jnp.float32
BF16 = jnp.bfloat16
CHUNKS = 4
STEPS = OWN // PAIR
VMEM_LIMIT = 24 * 1024 * 1024


@functools.cache
def tables():
    index = np.arange(ROWS)
    rate = index + 0.25
    angle = 2.0 * np.pi * rate[:, None] * index[None, :] / ROWS
    parts = np.concatenate([np.cos(angle), -np.sin(angle)])
    first = np.kron(parts, np.eye(SUB))
    last = first.T / TOKENS
    twist = 2.0 * np.pi * rate[:, None] * np.arange(COLS)[None, :] / TOKENS
    turn = 2.0 * np.pi * (np.arange(COLS)[:, None] * np.arange(COLS)[None, :] % COLS) / COLS
    cos, sin = np.cos(turn), np.sin(turn)
    ahead = np.block([[cos, -sin], [sin, cos]])
    back = np.block([[cos, sin], [-sin, cos]])
    kind = ml_dtypes.bfloat16
    return (
        np.stack([np.cos(twist), np.sin(twist)]).astype(np.float32),
        first.astype(kind),
        ahead.astype(kind),
        last.astype(kind),
        back.astype(kind),
    )


def dot(left, right):
    return jnp.dot(left, right, preferred_element_type=F32)


def both(left, right):
    return jnp.concatenate([left, right], axis=1)


def split_rows(block):
    wide = block.astype(F32)
    low = wide[:, :SUB].reshape(BLOCK, COLS)
    high = wide[:, SUB:].reshape(BLOCK, COLS)
    return both(low, high).astype(BF16)


def turns(twist_ref):
    spread = [jnp.broadcast_to(twist_ref[i][:, None, :], (ROWS, SUB, COLS)) for i in range(2)]
    return [table.reshape(BLOCK, COLS) for table in spread]


def spectra(blocks, twist_ref, first_ref, ahead_ref):
    cos, sin = turns(twist_ref)
    turned = []
    for rows in blocks:
        wide = dot(first_ref[...], rows)
        for side in range(2):
            lanes = slice(side * COLS, (side + 1) * COLS)
            real, imag = wide[:BLOCK, lanes], wide[BLOCK:, lanes]
            turned.append(both(real * cos + imag * sin, imag * cos - real * sin).astype(BF16))
    return dot(jnp.concatenate(turned, axis=0), ahead_ref[...])


def unturned(specs, twist_ref, back_ref):
    cos, sin = turns(twist_ref)
    wide = dot(specs.astype(BF16), back_ref[...])
    blocks = []
    for place in range(specs.shape[0] // (2 * BLOCK)):
        sides = []
        for side in range(2):
            low = (2 * place + side) * BLOCK
            real, imag = wide[low : low + BLOCK, :COLS], wide[low : low + BLOCK, COLS:]
            sides.append(jnp.concatenate([real * cos - imag * sin, imag * cos + real * sin], axis=0))
        blocks.append(both(*sides).astype(BF16))
    return blocks


def lags_of(rows, last_ref):
    wide = dot(last_ref[...], rows)
    shape = (ROWS, SUB, COLS)
    return jnp.concatenate([wide[:, :COLS].reshape(shape), wide[:, COLS:].reshape(shape)], axis=1)


def product(left, right, conj):
    left_re, left_im = left[:, :COLS].astype(F32), left[:, COLS:].astype(F32)
    right_re, right_im = right[:, :COLS].astype(F32), right[:, COLS:].astype(F32)
    if conj:
        return both(left_re * right_re + left_im * right_im, left_re * right_im - left_im * right_re)
    return both(left_re * right_re - left_im * right_im, left_re * right_im + left_im * right_re)


def copies_of(pairs, sems):
    copies = []
    for place, (source, target) in enumerate(pairs):
        copies.append(pltpu.make_async_copy(source, target, sems.at[place]))
    for copy in copies:
        copy.start()
    return copies


def wait_all(copies):
    for copy in copies:
        copy.wait()


def gate_kernel(query_hbm, key_hbm, value_hbm, cotan_hbm, out_hbm, held, sent, in_sems, out_sems):
    sources = (key_hbm, value_hbm, query_hbm, cotan_hbm)
    span = held.shape[2] // CHUNKS
    pairs = []
    for chunk in range(CHUNKS):
        lanes = pl.ds(chunk * span, span)
        pairs += [(source.at[:, lanes], held.at[place, :, lanes]) for place, source in enumerate(sources)]
    arriving = copies_of(pairs, in_sems)
    leaving = []
    for chunk in range(CHUNKS):
        wait_all(arriving[4 * chunk : 4 * chunk + 4])
        first_block, last_block = chunk * span // COLS, (chunk + 1) * span // COLS
        for block in range(first_block, last_block):
            lanes = pl.ds(block * COLS, COLS)
            for part in range(2):
                left, right = held[2 * part, :, lanes].astype(F32), held[2 * part + 1, :, lanes].astype(F32)
                turned = (left * right).T.astype(BF16)
                rows = slice(part * OWN, (part + 1) * OWN)
                sent[2 * block, rows] = turned[:OWN]
                sent[2 * block + 1, rows] = turned[OWN:]
        dests = pl.ds(2 * first_block, 2 * (last_block - first_block))
        copy = pltpu.make_async_copy(sent.at[dests], out_hbm.at[dests], out_sems.at[chunk])
        copy.start()
        leaving.append(copy)
    wait_all(leaving)


def filter_kernel(
    taps_hbm,
    twist_hbm,
    first_hbm,
    ahead_hbm,
    last_hbm,
    back_hbm,
    filt,
    twist,
    first,
    ahead,
    last,
    back,
    taps,
    sems,
):
    pairs = [(first_hbm, first), (twist_hbm, twist), (ahead_hbm, ahead), (taps_hbm, taps)]
    pairs += [(last_hbm, last), (back_hbm, back)]
    arriving = copies_of(pairs, sems)
    wait_all(arriving[:4])
    for step in range(STEPS):
        sides = []
        for side in range(2):
            low = (2 * step + side) * SUB
            sides.append(
                jnp.concatenate([taps[low : low + SUB, p * COLS : (p + 1) * COLS] for p in range(ROWS)], axis=0)
            )
        filt[step] = spectra([both(*sides).astype(BF16)], twist, first, ahead).astype(BF16)
    wait_all(arriving[4:])


def conv_kernel(data, filt, twist, first, ahead, last, back, out_hbm, cross_hbm, out, cross, out_sems):
    leaving = []
    for step in range(STEPS):
        blocks = []
        for part in range(2):
            rows = slice(part * OWN + step * PAIR, part * OWN + (step + 1) * PAIR)
            blocks.append(split_rows(data[:, rows, :]))
        specs = spectra(blocks, twist, first, ahead)
        gated, grads, turn = specs[: 2 * BLOCK], specs[2 * BLOCK :], filt[step]
        cross[step] = product(gated, grads, True).astype(BF16)
        leaving += copies_of([(cross.at[step], cross_hbm.at[step])], out_sems.at[step, 2:])
        prods = jnp.concatenate([product(turn, gated, False), product(turn, grads, True)], axis=0)
        for part, block in enumerate(unturned(prods, twist, back)):
            rows = slice(part * OWN + step * PAIR, part * OWN + (step + 1) * PAIR)
            out[:, rows, :] = lags_of(block, last).astype(BF16)
            leaving += copies_of([(out.at[:, rows, :], out_hbm.at[:, rows, :])], out_sems.at[step, part:])
    wait_all(leaving)


def taps_kernel(
    place_ref,
    cross_hbm,
    key_hbm,
    value_hbm,
    cotan_hbm,
    twist,
    last,
    back,
    own,
    near,
    keys,
    values,
    cotan,
    cross,
    lags_ref,
    sems,
    out_sems,
):
    pairs = [(cross_hbm, cross), (key_hbm, keys), (value_hbm, values), (cotan_hbm, cotan)]
    arriving = copies_of(pairs, sems)
    arriving[0].wait()
    per = ROWS // 4
    for step in range(STEPS):
        lags = lags_of(unturned(cross[step], twist, back)[0], last).astype(BF16)
        rows = slice(step * PAIR, (step + 1) * PAIR)
        for p in range(ROWS):
            lags_ref[p // per, rows, (p % per) * COLS : (p % per + 1) * COLS] = lags[p]
    place = place_ref[0]
    pairs = []
    for shift in range(4):
        target = (own, near)[shift % 2]
        pairs.append((lags_ref.at[jnp.bitwise_xor(place, shift)], target.at[shift // 2]))
    wait_all(copies_of(pairs, out_sems))
    wait_all(arriving[1:])


def mix_kernel(
    data, near, far, own, keys, values, cotan, query_out, key_out, value_out, filter_out, grads, total, out_sems
):
    span = keys.shape[1] // CHUNKS
    factors = (cotan, values, keys)
    outs = (query_out, key_out, value_out)
    whole = own[0].astype(F32) + near[0].astype(F32) + far[...].astype(F32)
    total[...] = whole * (1.0 / math.sqrt(4 * TOKENS))
    leaving = copies_of([(total, filter_out)], out_sems.at[CHUNKS])
    for chunk in range(CHUNKS):
        for block in range(chunk * span // COLS, (chunk + 1) * span // COLS):
            lanes = pl.ds(block * COLS, COLS)
            turned = []
            for part in range(2):
                rows = slice(part * OWN, (part + 1) * OWN)
                tall = jnp.concatenate([data[2 * block, rows], data[2 * block + 1, rows]], axis=0)
                turned.append(tall.astype(F32).T)
            conv, grad = turned
            for place, turn in enumerate((conv, grad, grad)):
                grads[place, :, lanes] = (turn * factors[place][:, lanes].astype(F32)).astype(BF16)
        lanes = pl.ds(chunk * span, span)
        pairs = [(grads.at[place, :, lanes], outs[place].at[:, lanes]) for place in range(3)]
        leaving += copies_of(pairs, out_sems.at[chunk])
    wait_all(leaving)


def call(kernel, out_shape, places, scratch=(), flops=0, nbytes=0):
    spaces = {"h": pltpu.HBM, "v": pltpu.VMEM, "s": pltpu.SMEM}
    specs = {"h": pl.BlockSpec(memory_space=pl.ANY)}
    specs |= {place: pl.BlockSpec(memory_space=spaces[place]) for place in "vs"}
    ins, outs = places.split()

    def run(*args):
        held = [pltpu.with_memory_space_constraint(x, spaces[p]) if p != "s" else x for x, p in zip(args, ins, strict=True)]
        return pl.pallas_call(
            kernel,
            out_shape=tuple(spaces[p](x.shape, x.dtype) for x, p in zip(out_shape, outs, strict=True)),
            in_specs=[specs[p] for p in ins],
            out_specs=tuple(specs[p] for p in outs),
            scratch_shapes=list(scratch),
            compiler_params=pltpu.CompilerParams(vmem_limit_bytes=VMEM_LIMIT),
            cost_estimate=pl.CostEstimate(flops=flops, bytes_accessed=nbytes, transcendentals=0),
        )(*held)

    return run


def swap(array):
    return lax.all_to_all(array, "seq", split_axis=0, concat_axis=0, tiled=True)


def on_device(query_in, key_in, value_in, grad_out, filter_taps):
    twist, first, ahead, last, back = (jnp.asarray(table) for table in tables())
    query, keys, values, cotan = query_in[0], key_in[0], value_in[0], grad_out[0]
    shape = jax.ShapeDtypeStruct
    sems = pltpu.SemaphoreType.DMA
    cube = shape((ROWS, 2 * OWN, COLS), BF16)
    filt_spec = shape((STEPS, 2 * BLOCK, 2 * COLS), BF16)
    wide = shape(query.shape, BF16)
    quarter = shape((OWN, TOKENS // 4), BF16)
    unit = 1 << 30

    def room(*arrays):
        return [pltpu.VMEM(array.shape, array.dtype) for array in arrays]

    (sent,) = call(
        gate_kernel,
        (cube,),
        "hhhh h",
        [pltpu.VMEM((4, *query.shape), BF16), *room(cube), sems((4 * CHUNKS,)), sems((CHUNKS,))],
        flops=1 << 20,
        nbytes=3 << 20,
    )(query, keys, values, cotan)
    filt, twist, first, ahead, last, back = call(
        filter_kernel,
        (filt_spec, twist, first, ahead, last, back),
        "hhhhhh vvvvvv",
        [*room(filter_taps), sems((6,))],
        flops=unit // 2,
        nbytes=3 << 20,
    )(filter_taps, twist, first, ahead, last, back)
    data = swap(sent)
    result, cross = call(
        conv_kernel,
        (cube, filt_spec),
        "vvvvvvv hh",
        [*room(cube, filt_spec), sems((STEPS, 3))],
        flops=2 * unit,
        nbytes=5 << 20,
    )(data, filt, twist, first, ahead, last, back)
    returned = swap(result)
    place = lax.axis_index("dp").astype(jnp.int32).reshape(1)
    half = shape((2, *quarter.shape), BF16)
    own, sent_near, keys, values, cotan = call(
        taps_kernel,
        (half, half, wide, wide, wide),
        "shhhhvvv vvvvv",
        [*room(filt_spec), pltpu.VMEM((4, *quarter.shape), BF16), sems((4,)), sems((4,))],
        flops=unit // 2,
        nbytes=3 << 20,
    )(place, cross, keys, values, cotan, twist, last, back)
    near = lax.ppermute(sent_near, "dp", [(d, d ^ 1) for d in range(4)])
    partial = (own[1].astype(F32) + near[1].astype(F32)).astype(BF16)
    far = lax.ppermute(partial, "dp", [(d, d ^ 2) for d in range(4)])
    grad_query, grad_key, grad_value, grad_filter = call(
        mix_kernel,
        (wide, wide, wide, shape(quarter.shape, F32)),
        "vvvvvvv hhhh",
        [pltpu.VMEM((3, *wide.shape), BF16), pltpu.VMEM(quarter.shape, F32), sems((CHUNKS + 1, 3))],
        flops=1 << 20,
        nbytes=4 << 20,
    )(returned, near, far, own, keys, values, cotan)
    return (grad_query[None], grad_key[None], grad_value[None], grad_filter)


def solution(mesh):
    tokens = P("dp", "seq", None)
    return jax.shard_map(
        on_device,
        mesh=mesh,
        in_specs=(tokens, tokens, tokens, tokens, P("seq", None)),
        out_specs=(tokens, tokens, tokens, P("seq", "dp")),
        check_vma=False,
    )
```

```python
import functools
import math

import jax
import jax.numpy as jnp
import ml_dtypes
import numpy as np
from jax import lax
from jax.experimental import pallas as pl
from jax.experimental.pallas import tpu as pltpu
from jax.sharding import PartitionSpec as P

TOKENS = 4096
ROWS = 32
COLS = 128
OWN = 64
SUB = 8
PAIR = 2 * SUB
BLOCK = ROWS * SUB
F32 = jnp.float32
BF16 = jnp.bfloat16
CHUNKS = 4
GATE_BLOCKS = (10, 6)
STEPS = OWN // PAIR
VMEM_LIMIT = 24 * 1024 * 1024


@functools.cache
def tables():
    index = np.arange(ROWS)
    rate = index + 0.25
    angle = 2.0 * np.pi * rate[:, None] * index[None, :] / ROWS
    parts = np.concatenate([np.cos(angle), -np.sin(angle)])
    first = np.kron(parts, np.eye(SUB))
    last = first.T / TOKENS
    twist = 2.0 * np.pi * rate[:, None] * np.arange(COLS)[None, :] / TOKENS
    turn = 2.0 * np.pi * (np.arange(COLS)[:, None] * np.arange(COLS)[None, :] % COLS) / COLS
    cos, sin = np.cos(turn), np.sin(turn)
    ahead = np.block([[cos, -sin], [sin, cos]])
    back = np.block([[cos, sin], [-sin, cos]])
    kind = ml_dtypes.bfloat16
    return (
        np.stack([np.cos(twist), np.sin(twist)]).astype(np.float32),
        first.astype(kind),
        ahead.astype(kind),
        last.astype(kind),
        back.astype(kind),
    )


def dot(left, right):
    return jnp.dot(left, right, preferred_element_type=F32)


def both(left, right):
    return jnp.concatenate([left, right], axis=1)


def split_rows(block):
    wide = block.astype(F32)
    low = wide[:, :SUB].reshape(BLOCK, COLS)
    high = wide[:, SUB:].reshape(BLOCK, COLS)
    return both(low, high).astype(BF16)


def turns(twist_ref):
    spread = [jnp.broadcast_to(twist_ref[i][:, None, :], (ROWS, SUB, COLS)) for i in range(2)]
    return [table.reshape(BLOCK, COLS) for table in spread]


def spectra(blocks, twist_ref, first_ref, ahead_ref):
    cos, sin = turns(twist_ref)
    turned = []
    for rows in blocks:
        wide = dot(first_ref[...], rows)
        for side in range(2):
            lanes = slice(side * COLS, (side + 1) * COLS)
            real, imag = wide[:BLOCK, lanes], wide[BLOCK:, lanes]
            turned.append(both(real * cos + imag * sin, imag * cos - real * sin).astype(BF16))
    return dot(jnp.concatenate(turned, axis=0), ahead_ref[...])


def unturned(specs, twist_ref, back_ref):
    cos, sin = turns(twist_ref)
    wide = dot(specs.astype(BF16), back_ref[...])
    blocks = []
    for place in range(specs.shape[0] // (2 * BLOCK)):
        sides = []
        for side in range(2):
            low = (2 * place + side) * BLOCK
            real, imag = wide[low : low + BLOCK, :COLS], wide[low : low + BLOCK, COLS:]
            sides.append(jnp.concatenate([real * cos - imag * sin, imag * cos + real * sin], axis=0))
        blocks.append(both(*sides).astype(BF16))
    return blocks


def lags_of(rows, last_ref):
    wide = dot(last_ref[...], rows)
    shape = (ROWS, SUB, COLS)
    return jnp.concatenate([wide[:, :COLS].reshape(shape), wide[:, COLS:].reshape(shape)], axis=1)


def product(left, right, conj):
    left_re, left_im = left[:, :COLS].astype(F32), left[:, COLS:].astype(F32)
    right_re, right_im = right[:, :COLS].astype(F32), right[:, COLS:].astype(F32)
    if conj:
        return both(left_re * right_re + left_im * right_im, left_re * right_im - left_im * right_re)
    return both(left_re * right_re - left_im * right_im, left_re * right_im + left_im * right_re)


def copies_of(pairs, sems):
    copies = []
    for place, (source, target) in enumerate(pairs):
        copies.append(pltpu.make_async_copy(source, target, sems.at[place]))
    for copy in copies:
        copy.start()
    return copies


def wait_all(copies):
    for copy in copies:
        copy.wait()


def gate_kernel(query_hbm, key_hbm, value_hbm, cotan_hbm, out_hbm, held, sent, in_sems, out_sems):
    sources = (key_hbm, value_hbm, query_hbm, cotan_hbm)
    pairs, starts = [], [sum(GATE_BLOCKS[:chunk]) for chunk in range(len(GATE_BLOCKS) + 1)]
    for low, high in zip(starts[:-1], starts[1:]):
        lanes = pl.ds(low * COLS, (high - low) * COLS)
        pairs += [(source.at[:, lanes], held.at[place, :, lanes]) for place, source in enumerate(sources)]
    arriving = copies_of(pairs, in_sems)
    leaving = []
    for chunk, (low, high) in enumerate(zip(starts[:-1], starts[1:])):
        wait_all(arriving[4 * chunk : 4 * chunk + 4])
        for block in range(low, high):
            lanes = pl.ds(block * COLS, COLS)
            for part in range(2):
                left, right = held[2 * part, :, lanes].astype(F32), held[2 * part + 1, :, lanes].astype(F32)
                turned = (left * right).T.astype(BF16)
                rows = slice(part * OWN, (part + 1) * OWN)
                sent[2 * block, rows] = turned[:OWN]
                sent[2 * block + 1, rows] = turned[OWN:]
        dests = pl.ds(2 * low, 2 * (high - low))
        copy = pltpu.make_async_copy(sent.at[dests], out_hbm.at[dests], out_sems.at[chunk])
        copy.start()
        leaving.append(copy)
    wait_all(leaving)


def filter_kernel(
    taps_hbm,
    twist_hbm,
    first_hbm,
    ahead_hbm,
    last_hbm,
    back_hbm,
    filt,
    twist,
    first,
    ahead,
    last,
    back,
    taps,
    sems,
):
    pairs = [(first_hbm, first), (twist_hbm, twist), (ahead_hbm, ahead), (taps_hbm, taps)]
    pairs += [(last_hbm, last), (back_hbm, back)]
    arriving = copies_of(pairs, sems)
    wait_all(arriving[:4])
    for step in range(STEPS):
        sides = []
        for side in range(2):
            low = (2 * step + side) * SUB
            sides.append(
                jnp.concatenate([taps[low : low + SUB, p * COLS : (p + 1) * COLS] for p in range(ROWS)], axis=0)
            )
        filt[step] = spectra([both(*sides).astype(BF16)], twist, first, ahead).astype(BF16)
    wait_all(arriving[4:])


def conv_kernel(data, filt, twist, first, ahead, last, back, out_hbm, cross_hbm, out, cross, out_sems):
    leaving = []
    prods = []
    for many in range(0, STEPS, 2):
        blocks = []
        for step in range(many, many + 2):
            for part in range(2):
                rows = slice(part * OWN + step * PAIR, part * OWN + (step + 1) * PAIR)
                blocks.append(split_rows(data[:, rows, :]))
        specs = spectra(blocks, twist, first, ahead)
        for step in range(many, many + 2):
            low = (step - many) * 4 * BLOCK
            gated, grads, turn = specs[low : low + 2 * BLOCK], specs[low + 2 * BLOCK : low + 4 * BLOCK], filt[step]
            cross[step] = product(gated, grads, True).astype(BF16)
            leaving += copies_of([(cross.at[step], cross_hbm.at[step])], out_sems.at[step, 2:])
            prods += [product(turn, gated, False).astype(BF16), product(turn, grads, True).astype(BF16)]
    for many in range(0, STEPS, 1):
        blocks = unturned(jnp.concatenate(prods[2 * many : 2 * (many + 1)], axis=0), twist, back)
        for place, block in enumerate(blocks):
            step, part = many + place // 2, place % 2
            rows = slice(part * OWN + step * PAIR, part * OWN + (step + 1) * PAIR)
            out[:, rows, :] = lags_of(block, last).astype(BF16)
            leaving += copies_of([(out.at[:, rows, :], out_hbm.at[:, rows, :])], out_sems.at[step, part:])
    wait_all(leaving)


def taps_kernel(
    place_ref,
    cross_hbm,
    key_hbm,
    value_hbm,
    cotan_hbm,
    twist,
    last,
    back,
    own,
    near,
    keys,
    values,
    cotan,
    cross,
    lags_ref,
    sems,
    out_sems,
):
    pairs = [(cross_hbm, cross), (key_hbm, keys), (value_hbm, values), (cotan_hbm, cotan)]
    arriving = copies_of(pairs, sems)
    arriving[0].wait()
    per = ROWS // 4
    for step in range(STEPS):
        lags = lags_of(unturned(cross[step], twist, back)[0], last).astype(BF16)
        rows = slice(step * PAIR, (step + 1) * PAIR)
        for p in range(ROWS):
            lags_ref[p // per, rows, (p % per) * COLS : (p % per + 1) * COLS] = lags[p]
    place = place_ref[0]
    pairs = []
    for shift in range(4):
        target = (own, near)[shift % 2]
        pairs.append((lags_ref.at[jnp.bitwise_xor(place, shift)], target.at[shift // 2]))
    wait_all(copies_of(pairs, out_sems))
    wait_all(arriving[1:])


def mix_kernel(
    data, near, far, own, keys, values, cotan, query_out, key_out, value_out, filter_out, grads, total, out_sems
):
    span = keys.shape[1] // CHUNKS
    factors = (cotan, values, keys)
    outs = (query_out, key_out, value_out)
    whole = own[0].astype(F32) + near[0].astype(F32) + far[...].astype(F32)
    total[...] = whole * (1.0 / math.sqrt(4 * TOKENS))
    leaving = copies_of([(total, filter_out)], out_sems.at[CHUNKS])
    for chunk in range(CHUNKS):
        for block in range(chunk * span // COLS, (chunk + 1) * span // COLS):
            lanes = pl.ds(block * COLS, COLS)
            turned = []
            for part in range(2):
                rows = slice(part * OWN, (part + 1) * OWN)
                tall = jnp.concatenate([data[2 * block, rows], data[2 * block + 1, rows]], axis=0)
                turned.append(tall.astype(F32).T)
            conv, grad = turned
            for place, turn in enumerate((conv, grad, grad)):
                grads[place, :, lanes] = (turn * factors[place][:, lanes].astype(F32)).astype(BF16)
        lanes = pl.ds(chunk * span, span)
        pairs = [(grads.at[place, :, lanes], outs[place].at[:, lanes]) for place in range(3)]
        leaving += copies_of(pairs, out_sems.at[chunk])
    wait_all(leaving)


def call(kernel, out_shape, places, scratch=(), flops=0, nbytes=0):
    spaces = {"h": pltpu.HBM, "v": pltpu.VMEM, "s": pltpu.SMEM}
    specs = {"h": pl.BlockSpec(memory_space=pl.ANY)}
    specs |= {place: pl.BlockSpec(memory_space=spaces[place]) for place in "vs"}
    ins, outs = places.split()

    def run(*args):
        held = [pltpu.with_memory_space_constraint(x, spaces[p]) if p != "s" else x for x, p in zip(args, ins, strict=True)]
        return pl.pallas_call(
            kernel,
            out_shape=tuple(spaces[p](x.shape, x.dtype) for x, p in zip(out_shape, outs, strict=True)),
            in_specs=[specs[p] for p in ins],
            out_specs=tuple(specs[p] for p in outs),
            scratch_shapes=list(scratch),
            compiler_params=pltpu.CompilerParams(vmem_limit_bytes=VMEM_LIMIT),
            cost_estimate=pl.CostEstimate(flops=flops, bytes_accessed=nbytes, transcendentals=0),
        )(*held)

    return run


def swap(array):
    return lax.all_to_all(array, "seq", split_axis=0, concat_axis=0, tiled=True)


def on_device(query_in, key_in, value_in, grad_out, filter_taps):
    twist, first, ahead, last, back = (jnp.asarray(table) for table in tables())
    query, keys, values, cotan = query_in[0], key_in[0], value_in[0], grad_out[0]
    shape = jax.ShapeDtypeStruct
    sems = pltpu.SemaphoreType.DMA
    cube = shape((ROWS, 2 * OWN, COLS), BF16)
    filt_spec = shape((STEPS, 2 * BLOCK, 2 * COLS), BF16)
    wide = shape(query.shape, BF16)
    quarter = shape((OWN, TOKENS // 4), BF16)
    unit = 1 << 30

    def room(*arrays):
        return [pltpu.VMEM(array.shape, array.dtype) for array in arrays]

    (sent,) = call(
        gate_kernel,
        (cube,),
        "hhhh h",
        [pltpu.VMEM((4, *query.shape), BF16), *room(cube), sems((4 * len(GATE_BLOCKS),)), sems((len(GATE_BLOCKS),))],
        flops=1 << 20,
        nbytes=3 << 20,
    )(query, keys, values, cotan)
    filt, twist, first, ahead, last, back = call(
        filter_kernel,
        (filt_spec, twist, first, ahead, last, back),
        "hhhhhh vvvvvv",
        [*room(filter_taps), sems((6,))],
        flops=unit // 2,
        nbytes=3 << 20,
    )(filter_taps, twist, first, ahead, last, back)
    data = swap(sent)
    result, cross = call(
        conv_kernel,
        (cube, filt_spec),
        "vvvvvvv hh",
        [*room(cube, filt_spec), sems((STEPS, 3))],
        flops=2 * unit,
        nbytes=5 << 20,
    )(data, filt, twist, first, ahead, last, back)
    returned = swap(result)
    place = lax.axis_index("dp").astype(jnp.int32).reshape(1)
    half = shape((2, *quarter.shape), BF16)
    own, sent_near, keys, values, cotan = call(
        taps_kernel,
        (half, half, wide, wide, wide),
        "shhhhvvv vvvvv",
        [*room(filt_spec), pltpu.VMEM((4, *quarter.shape), BF16), sems((4,)), sems((4,))],
        flops=unit // 2,
        nbytes=3 << 20,
    )(place, cross, keys, values, cotan, twist, last, back)
    near = lax.ppermute(sent_near, "dp", [(d, d ^ 1) for d in range(4)])
    partial = (own[1].astype(F32) + near[1].astype(F32)).astype(BF16)
    far = lax.ppermute(partial, "dp", [(d, d ^ 2) for d in range(4)])
    grad_query, grad_key, grad_value, grad_filter = call(
        mix_kernel,
        (wide, wide, wide, shape(quarter.shape, F32)),
        "vvvvvvv hhhh",
        [pltpu.VMEM((3, *wide.shape), BF16), pltpu.VMEM(quarter.shape, F32), sems((CHUNKS + 1, 3))],
        flops=1 << 20,
        nbytes=4 << 20,
    )(returned, near, far, own, keys, values, cotan)
    return (grad_query[None], grad_key[None], grad_value[None], grad_filter)


def solution(mesh):
    tokens = P("dp", "seq", None)
    return jax.shard_map(
        on_device,
        mesh=mesh,
        in_specs=(tokens, tokens, tokens, tokens, P("seq", None)),
        out_specs=(tokens, tokens, tokens, P("seq", "dp")),
        check_vma=False,
    )
```

```python
import functools
import math

import jax
import jax.numpy as jnp
import ml_dtypes
import numpy as np
from jax import lax
from jax.experimental import pallas as pl
from jax.experimental.pallas import tpu as pltpu
from jax.sharding import PartitionSpec as P

TOKENS = 4096
ROWS = 32
COLS = 128
OWN = 64
SUB = 8
PAIR = 2 * SUB
BLOCK = ROWS * SUB
F32 = jnp.float32
BF16 = jnp.bfloat16
CHUNKS = 4
GATE_BLOCKS = (10, 6)
LATE_CHUNKS = 4
STEPS = OWN // PAIR
VMEM_LIMIT = 24 * 1024 * 1024


@functools.cache
def tables():
    index = np.arange(ROWS)
    rate = index + 0.25
    angle = 2.0 * np.pi * rate[:, None] * index[None, :] / ROWS
    parts = np.concatenate([np.cos(angle), -np.sin(angle)])
    first = np.kron(parts, np.eye(SUB))
    last = first.T / TOKENS
    twist = 2.0 * np.pi * rate[:, None] * np.arange(COLS)[None, :] / TOKENS
    turn = 2.0 * np.pi * (np.arange(COLS)[:, None] * np.arange(COLS)[None, :] % COLS) / COLS
    cos, sin = np.cos(turn), np.sin(turn)
    ahead = np.block([[cos, -sin], [sin, cos]])
    back = np.block([[cos, sin], [-sin, cos]])
    kind = ml_dtypes.bfloat16
    return (
        np.stack([np.cos(twist), np.sin(twist)]).astype(np.float32),
        first.astype(kind),
        ahead.astype(kind),
        last.astype(kind),
        back.astype(kind),
    )


def dot(left, right):
    return jnp.dot(left, right, preferred_element_type=F32)


def both(left, right):
    return jnp.concatenate([left, right], axis=1)


def split_rows(block):
    wide = block.astype(F32)
    low = wide[:, :SUB].reshape(BLOCK, COLS)
    high = wide[:, SUB:].reshape(BLOCK, COLS)
    return both(low, high).astype(BF16)


def turns(twist_ref):
    spread = [jnp.broadcast_to(twist_ref[i][:, None, :], (ROWS, SUB, COLS)) for i in range(2)]
    return [table.reshape(BLOCK, COLS) for table in spread]


def spectra(blocks, twist_ref, first_ref, ahead_ref):
    cos, sin = turns(twist_ref)
    turned = []
    for rows in blocks:
        wide = dot(first_ref[...], rows)
        for side in range(2):
            lanes = slice(side * COLS, (side + 1) * COLS)
            real, imag = wide[:BLOCK, lanes], wide[BLOCK:, lanes]
            turned.append(both(real * cos + imag * sin, imag * cos - real * sin).astype(BF16))
    return dot(jnp.concatenate(turned, axis=0), ahead_ref[...])


def unturned(specs, twist_ref, back_ref):
    cos, sin = turns(twist_ref)
    wide = dot(specs.astype(BF16), back_ref[...])
    blocks = []
    for place in range(specs.shape[0] // (2 * BLOCK)):
        sides = []
        for side in range(2):
            low = (2 * place + side) * BLOCK
            real, imag = wide[low : low + BLOCK, :COLS], wide[low : low + BLOCK, COLS:]
            sides.append(jnp.concatenate([real * cos - imag * sin, imag * cos + real * sin], axis=0))
        blocks.append(both(*sides).astype(BF16))
    return blocks


def lags_of(rows, last_ref):
    wide = dot(last_ref[...], rows)
    shape = (ROWS, SUB, COLS)
    return jnp.concatenate([wide[:, :COLS].reshape(shape), wide[:, COLS:].reshape(shape)], axis=1)


def product(left, right, conj):
    left_re, left_im = left[:, :COLS].astype(F32), left[:, COLS:].astype(F32)
    right_re, right_im = right[:, :COLS].astype(F32), right[:, COLS:].astype(F32)
    if conj:
        return both(left_re * right_re + left_im * right_im, left_re * right_im - left_im * right_re)
    return both(left_re * right_re - left_im * right_im, left_re * right_im + left_im * right_re)


def copies_of(pairs, sems):
    copies = []
    for place, (source, target) in enumerate(pairs):
        copies.append(pltpu.make_async_copy(source, target, sems.at[place]))
    for copy in copies:
        copy.start()
    return copies


def wait_all(copies):
    for copy in copies:
        copy.wait()


def gate_blocks(held, sent, low, count):
    for place in range(count):
        block = low + place
        lanes = pl.ds(block * COLS if isinstance(block, int) else pl.multiple_of(block * COLS, COLS), COLS)
        for part in range(2):
            left, right = held[2 * part, :, lanes].astype(F32), held[2 * part + 1, :, lanes].astype(F32)
            turned = (left * right).T.astype(BF16)
            rows = slice(part * OWN, (part + 1) * OWN)
            sent[2 * block, rows] = turned[:OWN]
            sent[2 * block + 1, rows] = turned[OWN:]


def gate_kernel(place_ref, query_hbm, key_hbm, value_hbm, cotan_hbm, out_hbm, held, sent, in_sems, out_sems):
    sources = (key_hbm, value_hbm, query_hbm, cotan_hbm)
    core = jnp.bitwise_and(place_ref[0], 1)

    @pl.when(core == 1)
    def _():
        pairs, starts = [], [sum(GATE_BLOCKS[:chunk]) for chunk in range(len(GATE_BLOCKS) + 1)]
        for low, high in zip(starts[:-1], starts[1:]):
            lanes = pl.ds(low * COLS, (high - low) * COLS)
            pairs += [(source.at[:, lanes], held.at[place, :, lanes]) for place, source in enumerate(sources)]
        arriving = copies_of(pairs, in_sems)
        leaving = []
        for chunk, (low, high) in enumerate(zip(starts[:-1], starts[1:])):
            wait_all(arriving[4 * chunk : 4 * chunk + 4])
            gate_blocks(held, sent, low, high - low)
            dests = pl.ds(2 * low, 2 * (high - low))
            leaving += copies_of([(sent.at[dests], out_hbm.at[dests])], out_sems.at[chunk : chunk + 1])
        wait_all(leaving)

    @pl.when(core == 0)
    def _():
        count = held.shape[2] // COLS // LATE_CHUNKS

        @pl.loop(0, LATE_CHUNKS)
        def _(chunk):
            lanes = pl.ds(pl.multiple_of(chunk * count * COLS, COLS), count * COLS)
            pairs = [(source.at[:, lanes], held.at[place, :, lanes]) for place, source in enumerate(sources)]
            wait_all(copies_of(pairs, in_sems))
            gate_blocks(held, sent, chunk * count, count)
            dests = pl.ds(2 * chunk * count, 2 * count)
            wait_all(copies_of([(sent.at[dests], out_hbm.at[dests])], out_sems))


def filter_kernel(
    taps_hbm,
    twist_hbm,
    first_hbm,
    ahead_hbm,
    last_hbm,
    back_hbm,
    filt,
    twist,
    first,
    ahead,
    last,
    back,
    taps,
    sems,
):
    pairs = [(first_hbm, first), (twist_hbm, twist), (ahead_hbm, ahead), (taps_hbm, taps)]
    pairs += [(last_hbm, last), (back_hbm, back)]
    arriving = copies_of(pairs, sems)
    wait_all(arriving[:4])
    for step in range(STEPS):
        sides = []
        for side in range(2):
            low = (2 * step + side) * SUB
            sides.append(
                jnp.concatenate([taps[low : low + SUB, p * COLS : (p + 1) * COLS] for p in range(ROWS)], axis=0)
            )
        filt[step] = spectra([both(*sides).astype(BF16)], twist, first, ahead).astype(BF16)
    wait_all(arriving[4:])


def conv_kernel(place_ref, data, filt, twist, first, ahead, last, back, out_hbm, own, near, out, terms, out_sems):
    leaving = []
    prods, cross = [], []
    for many in range(0, STEPS, 2):
        blocks = []
        for step in range(many, many + 2):
            for part in range(2):
                rows = slice(part * OWN + step * PAIR, part * OWN + (step + 1) * PAIR)
                blocks.append(split_rows(data[:, rows, :]))
        specs = spectra(blocks, twist, first, ahead)
        for step in range(many, many + 2):
            low = (step - many) * 4 * BLOCK
            gated, grads, turn = specs[low : low + 2 * BLOCK], specs[low + 2 * BLOCK : low + 4 * BLOCK], filt[step]
            cross.append(product(gated, grads, True).astype(BF16))
            prods.append(jnp.concatenate([product(turn, gated, False), product(turn, grads, True)], axis=0).astype(BF16))
    for step in range(STEPS):
        for part, block in enumerate(unturned(prods[step], twist, back)):
            rows = slice(part * OWN + step * PAIR, part * OWN + (step + 1) * PAIR)
            out[:, rows, :] = lags_of(block, last).astype(BF16)
            leaving += copies_of([(out.at[:, rows, :], out_hbm.at[:, rows, :])], out_sems.at[step, part:])
    per = ROWS // 4
    for step in range(STEPS):
        (block,) = unturned(cross[step], twist, back)
        lags = lags_of(block, last).astype(BF16)
        rows = slice(step * PAIR, (step + 1) * PAIR)
        for p in range(ROWS):
            terms[p // per, rows, (p % per) * COLS : (p % per + 1) * COLS] = lags[p]
    place = place_ref[0]
    for shift in range(4):
        target = (own, near)[shift % 2]
        target[shift // 2] = terms[jnp.bitwise_xor(place, shift)]
    wait_all(leaving)


def bring_kernel(terms, key_hbm, value_hbm, cotan_hbm, own, keys, values, cotan, sems):
    copies = copies_of([(key_hbm, keys), (value_hbm, values), (cotan_hbm, cotan)], sems)
    own[...] = terms[0]
    wait_all(copies)


def mix_kernel(
    data, near, far, own, keys, values, cotan, query_out, key_out, value_out, filter_out, grads, total, out_sems
):
    span = keys.shape[1] // CHUNKS
    factors = (cotan, values, keys)
    outs = (query_out, key_out, value_out)
    whole = own[...].astype(F32) + near[0].astype(F32) + far[...].astype(F32)
    total[...] = whole * (1.0 / math.sqrt(4 * TOKENS))
    leaving = copies_of([(total, filter_out)], out_sems.at[CHUNKS])
    for chunk in range(CHUNKS):
        for block in range(chunk * span // COLS, (chunk + 1) * span // COLS):
            lanes = pl.ds(block * COLS, COLS)
            turned = []
            for part in range(2):
                rows = slice(part * OWN, (part + 1) * OWN)
                tall = jnp.concatenate([data[2 * block, rows], data[2 * block + 1, rows]], axis=0)
                turned.append(tall.astype(F32).T)
            conv, grad = turned
            for place, turn in enumerate((conv, grad, grad)):
                grads[place, :, lanes] = (turn * factors[place][:, lanes].astype(F32)).astype(BF16)
        lanes = pl.ds(chunk * span, span)
        pairs = [(grads.at[place, :, lanes], outs[place].at[:, lanes]) for place in range(3)]
        leaving += copies_of(pairs, out_sems.at[chunk])
    wait_all(leaving)


def call(kernel, out_shape, places, scratch=(), flops=0, nbytes=0):
    spaces = {"h": pltpu.HBM, "v": pltpu.VMEM, "s": pltpu.SMEM}
    specs = {"h": pl.BlockSpec(memory_space=pl.ANY)}
    specs |= {place: pl.BlockSpec(memory_space=spaces[place]) for place in "vs"}
    ins, outs = places.split()

    def run(*args):
        held = [pltpu.with_memory_space_constraint(x, spaces[p]) if p != "s" else x for x, p in zip(args, ins, strict=True)]
        return pl.pallas_call(
            kernel,
            out_shape=tuple(spaces[p](x.shape, x.dtype) for x, p in zip(out_shape, outs, strict=True)),
            in_specs=[specs[p] for p in ins],
            out_specs=tuple(specs[p] for p in outs),
            scratch_shapes=list(scratch),
            compiler_params=pltpu.CompilerParams(vmem_limit_bytes=VMEM_LIMIT),
            cost_estimate=pl.CostEstimate(flops=flops, bytes_accessed=nbytes, transcendentals=0),
        )(*held)

    return run


def swap(array):
    return lax.all_to_all(array, "seq", split_axis=0, concat_axis=0, tiled=True)


def on_device(query_in, key_in, value_in, grad_out, filter_taps):
    twist, first, ahead, last, back = (jnp.asarray(table) for table in tables())
    query, keys, values, cotan = query_in[0], key_in[0], value_in[0], grad_out[0]
    shape = jax.ShapeDtypeStruct
    sems = pltpu.SemaphoreType.DMA
    cube = shape((ROWS, 2 * OWN, COLS), BF16)
    filt_spec = shape((STEPS, 2 * BLOCK, 2 * COLS), BF16)
    wide = shape(query.shape, BF16)
    quarter = shape((OWN, TOKENS // 4), BF16)
    unit = 1 << 30

    def room(*arrays):
        return [pltpu.VMEM(array.shape, array.dtype) for array in arrays]

    place = lax.axis_index("dp").astype(jnp.int32).reshape(1)
    (sent,) = call(
        gate_kernel,
        (cube,),
        "shhhh h",
        [pltpu.VMEM((4, *query.shape), BF16), *room(cube), sems((4 * len(GATE_BLOCKS),)), sems((len(GATE_BLOCKS),))],
        flops=1 << 20,
        nbytes=3 << 20,
    )(place, query, keys, values, cotan)
    filt, twist, first, ahead, last, back = call(
        filter_kernel,
        (filt_spec, twist, first, ahead, last, back),
        "hhhhhh vvvvvv",
        [*room(filter_taps), sems((6,))],
        flops=unit // 2,
        nbytes=3 << 20,
    )(filter_taps, twist, first, ahead, last, back)
    data = swap(sent)
    half = shape((2, *quarter.shape), BF16)
    result, terms, sent_near = call(
        conv_kernel,
        (cube, half, half),
        "svvvvvvv hvv",
        [*room(cube), pltpu.VMEM((4, *quarter.shape), BF16), sems((STEPS, 2))],
        flops=2 * unit,
        nbytes=5 << 20,
    )(place, data, filt, twist, first, ahead, last, back)
    near = lax.ppermute(sent_near, "dp", [(d, d ^ 1) for d in range(4)])
    returned = swap(result)
    own, keys, values, cotan = call(
        bring_kernel,
        (quarter, wide, wide, wide),
        "vhhh vvvv",
        [sems((3,))],
        flops=1 << 20,
        nbytes=3 << 20,
    )(terms, keys, values, cotan)
    partial = (terms[1].astype(F32) + near[1].astype(F32)).astype(BF16)
    far = lax.ppermute(partial, "dp", [(d, d ^ 2) for d in range(4)])
    grad_query, grad_key, grad_value, grad_filter = call(
        mix_kernel,
        (wide, wide, wide, shape(quarter.shape, F32)),
        "vvvvvvv hhhh",
        [pltpu.VMEM((3, *wide.shape), BF16), pltpu.VMEM(quarter.shape, F32), sems((CHUNKS + 1, 3))],
        flops=1 << 20,
        nbytes=4 << 20,
    )(returned, near, far, own, keys, values, cotan)
    return (grad_query[None], grad_key[None], grad_value[None], grad_filter)


def solution(mesh):
    tokens = P("dp", "seq", None)
    return jax.shard_map(
        on_device,
        mesh=mesh,
        in_specs=(tokens, tokens, tokens, tokens, P("seq", None)),
        out_specs=(tokens, tokens, tokens, P("seq", "dp")),
        check_vma=False,
    )
```

```python
import functools
import math

import jax
import jax.numpy as jnp
import ml_dtypes
import numpy as np
from jax import lax
from jax.experimental import pallas as pl
from jax.experimental.pallas import tpu as pltpu
from jax.sharding import PartitionSpec as P

TOKENS = 4096
ROWS = 32
COLS = 128
OWN = 64
SUB = 8
PAIR = 2 * SUB
BLOCK = ROWS * SUB
F32 = jnp.float32
BF16 = jnp.bfloat16
CHUNKS = 4
GATE_BLOCKS = (10, 6)
LATE_BLOCKS = (6, 5, 5)
STEPS = OWN // PAIR
VMEM_LIMIT = 24 * 1024 * 1024


@functools.cache
def tables():
    index = np.arange(ROWS)
    rate = index + 0.25
    angle = 2.0 * np.pi * rate[:, None] * index[None, :] / ROWS
    parts = np.concatenate([np.cos(angle), -np.sin(angle)])
    first = np.kron(parts, np.eye(SUB))
    last = first.T / TOKENS
    twist = 2.0 * np.pi * rate[:, None] * np.arange(COLS)[None, :] / TOKENS
    turn = 2.0 * np.pi * (np.arange(COLS)[:, None] * np.arange(COLS)[None, :] % COLS) / COLS
    cos, sin = np.cos(turn), np.sin(turn)
    ahead = np.block([[cos, -sin], [sin, cos]])
    back = np.block([[cos, sin], [-sin, cos]])
    kind = ml_dtypes.bfloat16
    return (
        np.stack([np.cos(twist), np.sin(twist)]).astype(np.float32),
        first.astype(kind),
        ahead.astype(kind),
        last.astype(kind),
        back.astype(kind),
    )


def dot(left, right):
    return jnp.dot(left, right, preferred_element_type=F32)


def both(left, right):
    return jnp.concatenate([left, right], axis=1)


def split_rows(block):
    wide = block.astype(F32)
    low = wide[:, :SUB].reshape(BLOCK, COLS)
    high = wide[:, SUB:].reshape(BLOCK, COLS)
    return both(low, high).astype(BF16)


def turns(twist_ref):
    spread = [jnp.broadcast_to(twist_ref[i][:, None, :], (ROWS, SUB, COLS)) for i in range(2)]
    return [table.reshape(BLOCK, COLS) for table in spread]


def spectra(blocks, twist_ref, first_ref, ahead_ref):
    cos, sin = turns(twist_ref)
    turned = []
    for rows in blocks:
        wide = dot(first_ref[...], rows)
        for side in range(2):
            lanes = slice(side * COLS, (side + 1) * COLS)
            real, imag = wide[:BLOCK, lanes], wide[BLOCK:, lanes]
            turned.append(both(real * cos + imag * sin, imag * cos - real * sin).astype(BF16))
    return dot(jnp.concatenate(turned, axis=0), ahead_ref[...])


def unturned(specs, twist_ref, back_ref):
    cos, sin = turns(twist_ref)
    wide = dot(specs.astype(BF16), back_ref[...])
    blocks = []
    for place in range(specs.shape[0] // (2 * BLOCK)):
        sides = []
        for side in range(2):
            low = (2 * place + side) * BLOCK
            real, imag = wide[low : low + BLOCK, :COLS], wide[low : low + BLOCK, COLS:]
            sides.append(jnp.concatenate([real * cos - imag * sin, imag * cos + real * sin], axis=0))
        blocks.append(both(*sides).astype(BF16))
    return blocks


def lags_of(rows, last_ref):
    wide = dot(last_ref[...], rows)
    shape = (ROWS, SUB, COLS)
    return jnp.concatenate([wide[:, :COLS].reshape(shape), wide[:, COLS:].reshape(shape)], axis=1)


def product(left, right, conj):
    left_re, left_im = left[:, :COLS].astype(F32), left[:, COLS:].astype(F32)
    right_re, right_im = right[:, :COLS].astype(F32), right[:, COLS:].astype(F32)
    if conj:
        return both(left_re * right_re + left_im * right_im, left_re * right_im - left_im * right_re)
    return both(left_re * right_re - left_im * right_im, left_re * right_im + left_im * right_re)


def copies_of(pairs, sems):
    copies = []
    for place, (source, target) in enumerate(pairs):
        copies.append(pltpu.make_async_copy(source, target, sems.at[place]))
    for copy in copies:
        copy.start()
    return copies


def wait_all(copies):
    for copy in copies:
        copy.wait()


def gate_blocks(held, sent, low, count):
    for place in range(count):
        block = low + place
        lanes = pl.ds(block * COLS if isinstance(block, int) else pl.multiple_of(block * COLS, COLS), COLS)
        for part in range(2):
            left, right = held[2 * part, :, lanes].astype(F32), held[2 * part + 1, :, lanes].astype(F32)
            turned = (left * right).T.astype(BF16)
            rows = slice(part * OWN, (part + 1) * OWN)
            sent[2 * block, rows] = turned[:OWN]
            sent[2 * block + 1, rows] = turned[OWN:]


def gate_kernel(place_ref, query_hbm, key_hbm, value_hbm, cotan_hbm, out_hbm, held, sent, in_sems, out_sems):
    sources = (key_hbm, value_hbm, query_hbm, cotan_hbm)
    core = jnp.bitwise_and(place_ref[0], 1)

    @pl.when(core == 1)
    def _():
        pairs, starts = [], [sum(GATE_BLOCKS[:chunk]) for chunk in range(len(GATE_BLOCKS) + 1)]
        for low, high in zip(starts[:-1], starts[1:]):
            lanes = pl.ds(low * COLS, (high - low) * COLS)
            pairs += [(source.at[:, lanes], held.at[place, :, lanes]) for place, source in enumerate(sources)]
        arriving = copies_of(pairs, in_sems)
        leaving = []
        for chunk, (low, high) in enumerate(zip(starts[:-1], starts[1:])):
            wait_all(arriving[4 * chunk : 4 * chunk + 4])
            gate_blocks(held, sent, low, high - low)
            dests = pl.ds(2 * low, 2 * (high - low))
            leaving += copies_of([(sent.at[dests], out_hbm.at[dests])], out_sems.at[chunk : chunk + 1])
        wait_all(leaving)

    @pl.when(core == 0)
    def _():
        low = 0
        for count in LATE_BLOCKS:
            lanes = pl.ds(low * COLS, count * COLS)
            pairs = [(source.at[:, lanes], held.at[place, :, lanes]) for place, source in enumerate(sources)]
            wait_all(copies_of(pairs, in_sems))
            gate_blocks(held, sent, low, count)
            dests = pl.ds(2 * low, 2 * count)
            wait_all(copies_of([(sent.at[dests], out_hbm.at[dests])], out_sems))
            low += count


def filter_kernel(
    taps_hbm,
    twist_hbm,
    first_hbm,
    ahead_hbm,
    last_hbm,
    back_hbm,
    filt,
    twist,
    first,
    ahead,
    last,
    back,
    taps,
    sems,
):
    pairs = [(first_hbm, first), (twist_hbm, twist), (ahead_hbm, ahead), (taps_hbm, taps)]
    pairs += [(last_hbm, last), (back_hbm, back)]
    arriving = copies_of(pairs, sems)
    wait_all(arriving[:4])
    for step in range(STEPS):
        sides = []
        for side in range(2):
            low = (2 * step + side) * SUB
            sides.append(
                jnp.concatenate([taps[low : low + SUB, p * COLS : (p + 1) * COLS] for p in range(ROWS)], axis=0)
            )
        filt[step] = spectra([both(*sides).astype(BF16)], twist, first, ahead).astype(BF16)
    wait_all(arriving[4:])


def conv_kernel(place_ref, data, filt, twist, first, ahead, last, back, out_hbm, own, near, out, terms, out_sems):
    leaving = []
    prods, cross = [], []
    for many in range(0, STEPS, 2):
        blocks = []
        for step in range(many, many + 2):
            for part in range(2):
                rows = slice(part * OWN + step * PAIR, part * OWN + (step + 1) * PAIR)
                blocks.append(split_rows(data[:, rows, :]))
        specs = spectra(blocks, twist, first, ahead)
        for step in range(many, many + 2):
            low = (step - many) * 4 * BLOCK
            gated, grads, turn = specs[low : low + 2 * BLOCK], specs[low + 2 * BLOCK : low + 4 * BLOCK], filt[step]
            cross.append(product(gated, grads, True).astype(BF16))
            prods.append(jnp.concatenate([product(turn, gated, False), product(turn, grads, True)], axis=0).astype(BF16))
    for step in range(STEPS):
        for part, block in enumerate(unturned(prods[step], twist, back)):
            rows = slice(part * OWN + step * PAIR, part * OWN + (step + 1) * PAIR)
            out[:, rows, :] = lags_of(block, last).astype(BF16)
            leaving += copies_of([(out.at[:, rows, :], out_hbm.at[:, rows, :])], out_sems.at[step, part:])
    per = ROWS // 4
    for step in range(STEPS):
        (block,) = unturned(cross[step], twist, back)
        lags = lags_of(block, last).astype(BF16)
        rows = slice(step * PAIR, (step + 1) * PAIR)
        for p in range(ROWS):
            terms[p // per, rows, (p % per) * COLS : (p % per + 1) * COLS] = lags[p]
    place = place_ref[0]
    for shift in range(4):
        target = (own, near)[shift % 2]
        target[shift // 2] = terms[jnp.bitwise_xor(place, shift)]
    wait_all(leaving)


def bring_kernel(terms, key_hbm, value_hbm, cotan_hbm, own, keys, values, cotan, sems):
    copies = copies_of([(key_hbm, keys), (value_hbm, values), (cotan_hbm, cotan)], sems)
    own[...] = terms[0]
    wait_all(copies)


def mix_kernel(
    data, near, far, own, keys, values, cotan, query_out, key_out, value_out, filter_out, grads, total, out_sems
):
    span = keys.shape[1] // CHUNKS
    factors = (cotan, values, keys)
    outs = (query_out, key_out, value_out)
    whole = own[...].astype(F32) + near[0].astype(F32) + far[...].astype(F32)
    total[...] = whole * (1.0 / math.sqrt(4 * TOKENS))
    leaving = copies_of([(total, filter_out)], out_sems.at[CHUNKS])
    for chunk in range(CHUNKS):
        for block in range(chunk * span // COLS, (chunk + 1) * span // COLS):
            lanes = pl.ds(block * COLS, COLS)
            turned = []
            for part in range(2):
                rows = slice(part * OWN, (part + 1) * OWN)
                tall = jnp.concatenate([data[2 * block, rows], data[2 * block + 1, rows]], axis=0)
                turned.append(tall.astype(F32).T)
            conv, grad = turned
            for place, turn in enumerate((conv, grad, grad)):
                grads[place, :, lanes] = (turn * factors[place][:, lanes].astype(F32)).astype(BF16)
        lanes = pl.ds(chunk * span, span)
        pairs = [(grads.at[place, :, lanes], outs[place].at[:, lanes]) for place in range(3)]
        leaving += copies_of(pairs, out_sems.at[chunk])
    wait_all(leaving)


def call(kernel, out_shape, places, scratch=(), flops=0, nbytes=0):
    spaces = {"h": pltpu.HBM, "v": pltpu.VMEM, "s": pltpu.SMEM}
    specs = {"h": pl.BlockSpec(memory_space=pl.ANY)}
    specs |= {place: pl.BlockSpec(memory_space=spaces[place]) for place in "vs"}
    ins, outs = places.split()

    def run(*args):
        held = [pltpu.with_memory_space_constraint(x, spaces[p]) if p != "s" else x for x, p in zip(args, ins, strict=True)]
        return pl.pallas_call(
            kernel,
            out_shape=tuple(spaces[p](x.shape, x.dtype) for x, p in zip(out_shape, outs, strict=True)),
            in_specs=[specs[p] for p in ins],
            out_specs=tuple(specs[p] for p in outs),
            scratch_shapes=list(scratch),
            compiler_params=pltpu.CompilerParams(vmem_limit_bytes=VMEM_LIMIT),
            cost_estimate=pl.CostEstimate(flops=flops, bytes_accessed=nbytes, transcendentals=0),
        )(*held)

    return run


def swap(array):
    return lax.all_to_all(array, "seq", split_axis=0, concat_axis=0, tiled=True)


def on_device(query_in, key_in, value_in, grad_out, filter_taps):
    twist, first, ahead, last, back = (jnp.asarray(table) for table in tables())
    query, keys, values, cotan = query_in[0], key_in[0], value_in[0], grad_out[0]
    shape = jax.ShapeDtypeStruct
    sems = pltpu.SemaphoreType.DMA
    cube = shape((ROWS, 2 * OWN, COLS), BF16)
    filt_spec = shape((STEPS, 2 * BLOCK, 2 * COLS), BF16)
    wide = shape(query.shape, BF16)
    quarter = shape((OWN, TOKENS // 4), BF16)
    unit = 1 << 30

    def room(*arrays):
        return [pltpu.VMEM(array.shape, array.dtype) for array in arrays]

    place = lax.axis_index("dp").astype(jnp.int32).reshape(1)
    (sent,) = call(
        gate_kernel,
        (cube,),
        "shhhh h",
        [pltpu.VMEM((4, *query.shape), BF16), *room(cube), sems((4 * len(GATE_BLOCKS),)), sems((len(GATE_BLOCKS),))],
        flops=1 << 20,
        nbytes=3 << 20,
    )(place, query, keys, values, cotan)
    filt, twist, first, ahead, last, back = call(
        filter_kernel,
        (filt_spec, twist, first, ahead, last, back),
        "hhhhhh vvvvvv",
        [*room(filter_taps), sems((6,))],
        flops=unit // 2,
        nbytes=3 << 20,
    )(filter_taps, twist, first, ahead, last, back)
    data = swap(sent)
    half = shape((2, *quarter.shape), BF16)
    result, terms, sent_near = call(
        conv_kernel,
        (cube, half, half),
        "svvvvvvv hvv",
        [*room(cube), pltpu.VMEM((4, *quarter.shape), BF16), sems((STEPS, 2))],
        flops=2 * unit,
        nbytes=5 << 20,
    )(place, data, filt, twist, first, ahead, last, back)
    near = lax.ppermute(sent_near, "dp", [(d, d ^ 1) for d in range(4)])
    returned = swap(result)
    own, keys, values, cotan = call(
        bring_kernel,
        (quarter, wide, wide, wide),
        "vhhh vvvv",
        [sems((3,))],
        flops=1 << 20,
        nbytes=3 << 20,
    )(terms, keys, values, cotan)
    partial = (terms[1].astype(F32) + near[1].astype(F32)).astype(BF16)
    far = lax.ppermute(partial, "dp", [(d, d ^ 2) for d in range(4)])
    grad_query, grad_key, grad_value, grad_filter = call(
        mix_kernel,
        (wide, wide, wide, shape(quarter.shape, F32)),
        "vvvvvvv hhhh",
        [pltpu.VMEM((3, *wide.shape), BF16), pltpu.VMEM(quarter.shape, F32), sems((CHUNKS + 1, 3))],
        flops=1 << 20,
        nbytes=4 << 20,
    )(returned, near, far, own, keys, values, cotan)
    return (grad_query[None], grad_key[None], grad_value[None], grad_filter)


def solution(mesh):
    tokens = P("dp", "seq", None)
    return jax.shard_map(
        on_device,
        mesh=mesh,
        in_specs=(tokens, tokens, tokens, tokens, P("seq", None)),
        out_specs=(tokens, tokens, tokens, P("seq", "dp")),
        check_vma=False,
    )
```

```python
import functools
import math

import jax
import jax.numpy as jnp
import ml_dtypes
import numpy as np
from jax import lax
from jax.experimental import pallas as pl
from jax.experimental.pallas import tpu as pltpu
from jax.sharding import PartitionSpec as P

TOKENS = 4096
ROWS = 32
COLS = 128
OWN = 64
SUB = 8
PAIR = 2 * SUB
BLOCK = ROWS * SUB
F32 = jnp.float32
BF16 = jnp.bfloat16
CHUNKS = 4
GATE_BLOCKS = (10, 6)
LATE_BLOCKS = (6, 5, 5)
STEPS = OWN // PAIR
VMEM_LIMIT = 24 * 1024 * 1024


@functools.cache
def tables():
    index = np.arange(ROWS)
    rate = index + 0.25
    angle = 2.0 * np.pi * rate[:, None] * index[None, :] / ROWS
    parts = np.concatenate([np.cos(angle), -np.sin(angle)])
    first = np.kron(parts, np.eye(SUB))
    last = first.T / TOKENS
    twist = 2.0 * np.pi * rate[:, None] * np.arange(COLS)[None, :] / TOKENS
    turn = 2.0 * np.pi * (np.arange(COLS)[:, None] * np.arange(COLS)[None, :] % COLS) / COLS
    cos, sin = np.cos(turn), np.sin(turn)
    ahead = np.block([[cos, -sin], [sin, cos]])
    back = np.block([[cos, sin], [-sin, cos]])
    kind = ml_dtypes.bfloat16
    return (
        np.stack([np.cos(twist), np.sin(twist)]).astype(np.float32),
        first.astype(kind),
        ahead.astype(kind),
        last.astype(kind),
        back.astype(kind),
    )


def dot(left, right):
    return jnp.dot(left, right, preferred_element_type=F32)


def both(left, right):
    return jnp.concatenate([left, right], axis=1)


def split_rows(block):
    wide = block.astype(F32)
    low = wide[:, :SUB].reshape(BLOCK, COLS)
    high = wide[:, SUB:].reshape(BLOCK, COLS)
    return both(low, high).astype(BF16)


def turns(twist_ref):
    spread = [jnp.broadcast_to(twist_ref[i][:, None, :], (ROWS, SUB, COLS)) for i in range(2)]
    return [table.reshape(BLOCK, COLS) for table in spread]


def spectra(blocks, twist_ref, first_ref, ahead_ref):
    cos, sin = turns(twist_ref)
    turned = []
    for rows in blocks:
        wide = dot(first_ref[...], rows)
        for side in range(2):
            lanes = slice(side * COLS, (side + 1) * COLS)
            real, imag = wide[:BLOCK, lanes], wide[BLOCK:, lanes]
            turned.append(both(real * cos + imag * sin, imag * cos - real * sin).astype(BF16))
    return dot(jnp.concatenate(turned, axis=0), ahead_ref[...])


def unturned(specs, twist_ref, back_ref):
    cos, sin = turns(twist_ref)
    wide = dot(specs.astype(BF16), back_ref[...])
    blocks = []
    for place in range(specs.shape[0] // (2 * BLOCK)):
        sides = []
        for side in range(2):
            low = (2 * place + side) * BLOCK
            real, imag = wide[low : low + BLOCK, :COLS], wide[low : low + BLOCK, COLS:]
            sides.append(jnp.concatenate([real * cos - imag * sin, imag * cos + real * sin], axis=0))
        blocks.append(both(*sides).astype(BF16))
    return blocks


def lags_of(rows, last_ref):
    wide = dot(last_ref[...], rows)
    shape = (ROWS, SUB, COLS)
    return jnp.concatenate([wide[:, :COLS].reshape(shape), wide[:, COLS:].reshape(shape)], axis=1)


def product(left, right, conj):
    left_re, left_im = left[:, :COLS].astype(F32), left[:, COLS:].astype(F32)
    right_re, right_im = right[:, :COLS].astype(F32), right[:, COLS:].astype(F32)
    if conj:
        return both(left_re * right_re + left_im * right_im, left_re * right_im - left_im * right_re)
    return both(left_re * right_re - left_im * right_im, left_re * right_im + left_im * right_re)


def copies_of(pairs, sems):
    copies = []
    for place, (source, target) in enumerate(pairs):
        copies.append(pltpu.make_async_copy(source, target, sems.at[place]))
    for copy in copies:
        copy.start()
    return copies


def wait_all(copies):
    for copy in copies:
        copy.wait()


def gate_blocks(held, sent, low, count):
    for place in range(count):
        block = low + place
        lanes = pl.ds(block * COLS if isinstance(block, int) else pl.multiple_of(block * COLS, COLS), COLS)
        for part in range(2):
            left, right = held[2 * part, :, lanes].astype(F32), held[2 * part + 1, :, lanes].astype(F32)
            turned = (left * right).T.astype(BF16)
            rows = slice(part * OWN, (part + 1) * OWN)
            sent[2 * block, rows] = turned[:OWN]
            sent[2 * block + 1, rows] = turned[OWN:]


def gate_kernel(place_ref, query_hbm, key_hbm, value_hbm, cotan_hbm, out_hbm, held, sent, in_sems, out_sems):
    sources = (key_hbm, value_hbm, query_hbm, cotan_hbm)
    core = jnp.bitwise_and(place_ref[0], 1)

    @pl.when(core == 1)
    def _():
        pairs, starts = [], [sum(GATE_BLOCKS[:chunk]) for chunk in range(len(GATE_BLOCKS) + 1)]
        for low, high in zip(starts[:-1], starts[1:]):
            lanes = pl.ds(low * COLS, (high - low) * COLS)
            pairs += [(source.at[:, lanes], held.at[place, :, lanes]) for place, source in enumerate(sources)]
        arriving = copies_of(pairs, in_sems)
        leaving = []
        for chunk, (low, high) in enumerate(zip(starts[:-1], starts[1:])):
            wait_all(arriving[4 * chunk : 4 * chunk + 4])
            gate_blocks(held, sent, low, high - low)
            dests = pl.ds(2 * low, 2 * (high - low))
            leaving += copies_of([(sent.at[dests], out_hbm.at[dests])], out_sems.at[chunk : chunk + 1])
        wait_all(leaving)

    @pl.when(core == 0)
    def _():
        low = 0
        for count in LATE_BLOCKS:
            lanes = pl.ds(low * COLS, count * COLS)
            pairs = [(source.at[:, lanes], held.at[place, :, lanes]) for place, source in enumerate(sources)]
            wait_all(copies_of(pairs, in_sems))
            gate_blocks(held, sent, low, count)
            dests = pl.ds(2 * low, 2 * count)
            wait_all(copies_of([(sent.at[dests], out_hbm.at[dests])], out_sems))
            low += count


def filter_kernel(
    taps_hbm,
    twist_hbm,
    first_hbm,
    ahead_hbm,
    last_hbm,
    back_hbm,
    filt,
    twist,
    first,
    ahead,
    last,
    back,
    taps,
    sems,
):
    pairs = [(first_hbm, first), (twist_hbm, twist), (ahead_hbm, ahead), (taps_hbm, taps)]
    pairs += [(last_hbm, last), (back_hbm, back)]
    arriving = copies_of(pairs, sems)
    wait_all(arriving[:4])
    for step in range(STEPS):
        sides = []
        for side in range(2):
            low = (2 * step + side) * SUB
            sides.append(
                jnp.concatenate([taps[low : low + SUB, p * COLS : (p + 1) * COLS] for p in range(ROWS)], axis=0)
            )
        filt[step] = spectra([both(*sides).astype(BF16)], twist, first, ahead).astype(BF16)
    wait_all(arriving[4:])


def conv_kernel(place_ref, data, filt, twist, first, ahead, last, back, out_hbm, own, near, out, terms, out_sems):
    leaving = []
    prods, cross = [], []
    for many in range(0, STEPS, 4):
        blocks = []
        for step in range(many, many + 4):
            for part in range(2):
                rows = slice(part * OWN + step * PAIR, part * OWN + (step + 1) * PAIR)
                blocks.append(split_rows(data[:, rows, :]))
        specs = spectra(blocks, twist, first, ahead)
        for step in range(many, many + 4):
            low = (step - many) * 4 * BLOCK
            gated, grads, turn = specs[low : low + 2 * BLOCK], specs[low + 2 * BLOCK : low + 4 * BLOCK], filt[step]
            cross.append(product(gated, grads, True).astype(BF16))
            prods.append(jnp.concatenate([product(turn, gated, False), product(turn, grads, True)], axis=0).astype(BF16))
    for step in range(STEPS):
        for part, block in enumerate(unturned(prods[step], twist, back)):
            rows = slice(part * OWN + step * PAIR, part * OWN + (step + 1) * PAIR)
            out[:, rows, :] = lags_of(block, last).astype(BF16)
            leaving += copies_of([(out.at[:, rows, :], out_hbm.at[:, rows, :])], out_sems.at[step, part:])
    per = ROWS // 4
    for step in range(STEPS):
        (block,) = unturned(cross[step], twist, back)
        lags = lags_of(block, last).astype(BF16)
        rows = slice(step * PAIR, (step + 1) * PAIR)
        for p in range(ROWS):
            terms[p // per, rows, (p % per) * COLS : (p % per + 1) * COLS] = lags[p]
    place = place_ref[0]
    for shift in range(4):
        target = (own, near)[shift % 2]
        target[shift // 2] = terms[jnp.bitwise_xor(place, shift)]
    wait_all(leaving)


def bring_kernel(terms, key_hbm, value_hbm, cotan_hbm, own, keys, values, cotan, sems):
    copies = copies_of([(key_hbm, keys), (value_hbm, values), (cotan_hbm, cotan)], sems)
    own[...] = terms[0]
    wait_all(copies)


def mix_kernel(
    data, near, far, own, keys, values, cotan, query_out, key_out, value_out, filter_out, grads, total, out_sems
):
    span = keys.shape[1] // CHUNKS
    factors = (cotan, values, keys)
    outs = (query_out, key_out, value_out)
    whole = own[...].astype(F32) + near[0].astype(F32) + far[...].astype(F32)
    total[...] = whole * (1.0 / math.sqrt(4 * TOKENS))
    leaving = copies_of([(total, filter_out)], out_sems.at[CHUNKS])
    for chunk in range(CHUNKS):
        for block in range(chunk * span // COLS, (chunk + 1) * span // COLS):
            lanes = pl.ds(block * COLS, COLS)
            turned = []
            for part in range(2):
                rows = slice(part * OWN, (part + 1) * OWN)
                tall = jnp.concatenate([data[2 * block, rows], data[2 * block + 1, rows]], axis=0)
                turned.append(tall.astype(F32).T)
            conv, grad = turned
            for place, turn in enumerate((conv, grad, grad)):
                grads[place, :, lanes] = (turn * factors[place][:, lanes].astype(F32)).astype(BF16)
        lanes = pl.ds(chunk * span, span)
        pairs = [(grads.at[place, :, lanes], outs[place].at[:, lanes]) for place in range(3)]
        leaving += copies_of(pairs, out_sems.at[chunk])
    wait_all(leaving)


def call(kernel, out_shape, places, scratch=(), flops=0, nbytes=0):
    spaces = {"h": pltpu.HBM, "v": pltpu.VMEM, "s": pltpu.SMEM}
    specs = {"h": pl.BlockSpec(memory_space=pl.ANY)}
    specs |= {place: pl.BlockSpec(memory_space=spaces[place]) for place in "vs"}
    ins, outs = places.split()

    def run(*args):
        held = [pltpu.with_memory_space_constraint(x, spaces[p]) if p != "s" else x for x, p in zip(args, ins, strict=True)]
        return pl.pallas_call(
            kernel,
            out_shape=tuple(spaces[p](x.shape, x.dtype) for x, p in zip(out_shape, outs, strict=True)),
            in_specs=[specs[p] for p in ins],
            out_specs=tuple(specs[p] for p in outs),
            scratch_shapes=list(scratch),
            compiler_params=pltpu.CompilerParams(vmem_limit_bytes=VMEM_LIMIT),
            cost_estimate=pl.CostEstimate(flops=flops, bytes_accessed=nbytes, transcendentals=0),
        )(*held)

    return run


def swap(array):
    return lax.all_to_all(array, "seq", split_axis=0, concat_axis=0, tiled=True)


def on_device(query_in, key_in, value_in, grad_out, filter_taps):
    twist, first, ahead, last, back = (jnp.asarray(table) for table in tables())
    query, keys, values, cotan = query_in[0], key_in[0], value_in[0], grad_out[0]
    shape = jax.ShapeDtypeStruct
    sems = pltpu.SemaphoreType.DMA
    cube = shape((ROWS, 2 * OWN, COLS), BF16)
    filt_spec = shape((STEPS, 2 * BLOCK, 2 * COLS), BF16)
    wide = shape(query.shape, BF16)
    quarter = shape((OWN, TOKENS // 4), BF16)
    unit = 1 << 30

    def room(*arrays):
        return [pltpu.VMEM(array.shape, array.dtype) for array in arrays]

    place = lax.axis_index("dp").astype(jnp.int32).reshape(1)
    (sent,) = call(
        gate_kernel,
        (cube,),
        "shhhh h",
        [pltpu.VMEM((4, *query.shape), BF16), *room(cube), sems((4 * len(GATE_BLOCKS),)), sems((len(GATE_BLOCKS),))],
        flops=1 << 20,
        nbytes=3 << 20,
    )(place, query, keys, values, cotan)
    filt, twist, first, ahead, last, back = call(
        filter_kernel,
        (filt_spec, twist, first, ahead, last, back),
        "hhhhhh vvvvvv",
        [*room(filter_taps), sems((6,))],
        flops=unit // 2,
        nbytes=3 << 20,
    )(filter_taps, twist, first, ahead, last, back)
    data = swap(sent)
    half = shape((2, *quarter.shape), BF16)
    result, terms, sent_near = call(
        conv_kernel,
        (cube, half, half),
        "svvvvvvv hvv",
        [*room(cube), pltpu.VMEM((4, *quarter.shape), BF16), sems((STEPS, 2))],
        flops=2 * unit,
        nbytes=5 << 20,
    )(place, data, filt, twist, first, ahead, last, back)
    near = lax.ppermute(sent_near, "dp", [(d, d ^ 1) for d in range(4)])
    returned = swap(result)
    own, keys, values, cotan = call(
        bring_kernel,
        (quarter, wide, wide, wide),
        "vhhh vvvv",
        [sems((3,))],
        flops=1 << 20,
        nbytes=3 << 20,
    )(terms, keys, values, cotan)
    partial = (terms[1].astype(F32) + near[1].astype(F32)).astype(BF16)
    far = lax.ppermute(partial, "dp", [(d, d ^ 2) for d in range(4)])
    grad_query, grad_key, grad_value, grad_filter = call(
        mix_kernel,
        (wide, wide, wide, shape(quarter.shape, F32)),
        "vvvvvvv hhhh",
        [pltpu.VMEM((3, *wide.shape), BF16), pltpu.VMEM(quarter.shape, F32), sems((CHUNKS + 1, 3))],
        flops=1 << 20,
        nbytes=4 << 20,
    )(returned, near, far, own, keys, values, cotan)
    return (grad_query[None], grad_key[None], grad_value[None], grad_filter)


def solution(mesh):
    tokens = P("dp", "seq", None)
    return jax.shard_map(
        on_device,
        mesh=mesh,
        in_specs=(tokens, tokens, tokens, tokens, P("seq", None)),
        out_specs=(tokens, tokens, tokens, P("seq", "dp")),
        check_vma=False,
    )
```
